256 devices in a mesh: dp: 64 (over z, x, core), proto: 4 (over y).
Axes of the slice: x: 4, y: 4, z: 8, core: 2. Of those that a mesh axis runs over, the one named last changes fastest.
Arguments:
- student_feat: bfloat16 [16384, 256], P('dp')
- teacher_feat: bfloat16 [16384, 256], P('dp')
- proto_weight: float32 [65536, 256], P(('proto', 'dp'))
Outputs:
- grad_student: float32 [16384, 256], P('dp')
- grad_proto: float32 [65536, 256], P(('proto', 'dp'))
- loss: float32 [], replicated
All inputs are finite; a program needn't handle non-finite values.
Results may differ from the reference program's by a relative error of at most 0.0024.
Values may be sent and summed in bfloat16 or wider, within the bound.
A program may use at most 128 MiB of HBM per device.

```python
import jax
import jax.numpy as jnp
from jax import lax

BOT = 256
PROTOS = 65536
SWEEPS = 3
CROPS = 16384


def shared_direction(key):
    return jax.random.normal(key, (BOT,), jnp.float32)


def draw_proto_weight(key, part):
    direction = shared_direction(key)
    key = jax.random.fold_in(key, 11)
    noise_key, align_key = jax.random.split(key, 2)
    position = jnp.arange(PROTOS, dtype=jnp.float32)[:, None] / PROTOS
    noise_part = jax.random.normal(noise_key, (PROTOS, BOT), jnp.float32)
    rising = 0.3 + 2.7 * position
    alignment = jax.random.uniform(align_key, (PROTOS, 1), jnp.float32, -1.0, 1.0) * rising
    return (noise_part + alignment * direction[None, :]).astype(jnp.float32)


def draw_teacher_feat(key, part):
    direction = shared_direction(key)
    key = jax.random.fold_in(key, 12)
    noise_key, align_key = jax.random.split(key, 2)
    noise_part = jax.random.normal(noise_key, (CROPS, BOT), jnp.float32)
    rising = 0.5 + 1.5 * jnp.arange(CROPS, dtype=jnp.float32)[:, None] / CROPS
    alignment = jax.random.uniform(align_key, (CROPS, 1), jnp.float32, -1.0, 1.0) * rising
    return (noise_part + alignment * direction[None, :]).astype(jnp.bfloat16)


def draw_student_feat(key, part):
    direction = shared_direction(key)
    key = jax.random.fold_in(key, 13)
    noise_key, align_key = jax.random.split(key, 2)
    noise_part = jax.random.normal(noise_key, (CROPS, BOT), jnp.float32)
    rising = 0.5 + 1.5 * jnp.arange(CROPS, dtype=jnp.float32)[:, None] / CROPS
    alignment = jax.random.uniform(align_key, (CROPS, 1), jnp.float32, -1.0, 1.0) * rising
    return (noise_part + alignment * direction[None, :]).astype(jnp.bfloat16)


def setup_inputs(seed: int = 0) -> dict:
    streams_of = jax.random.split(jax.random.key(seed), 4)
    return {
        "student_feat": draw_student_feat(jax.random.fold_in(streams_of[3], 71), 0),
        "teacher_feat": draw_teacher_feat(jax.random.fold_in(streams_of[3], 71), 0),
        "proto_weight": draw_proto_weight(jax.random.fold_in(streams_of[3], 71), 0),
    }


teacher_temp = 0.04
student_temp = 0.1
loss_scale = 1024.0
epsilon = 1e-06
precise = lax.Precision.HIGHEST

def unit_rows(values):
    wide_values = values.astype(jnp.float32)
    return wide_values * lax.rsqrt(lax.optimization_barrier(jnp.sum(wide_values * wide_values, axis=1, keepdims=True)) + epsilon)

def unit_back(values, upstream):
    wide_values = values.astype(jnp.float32)
    inverse = lax.rsqrt(lax.optimization_barrier(jnp.sum(wide_values * wide_values, axis=1, keepdims=True)) + epsilon)
    direction = wide_values * inverse
    return (upstream - direction * lax.optimization_barrier(jnp.sum(direction * upstream, axis=1, keepdims=True))) * inverse

def logits_block(units, proto_block, temper):
    return jnp.dot(units.astype(jnp.float32), proto_block.astype(jnp.float32).T, precision=precise) / temper

def reference(student_feat, teacher_feat, proto_weight):
    student_unit = unit_rows(student_feat).astype(jnp.bfloat16)
    teacher_unit = unit_rows(teacher_feat).astype(jnp.bfloat16)
    proto_unit = unit_rows(proto_weight).astype(jnp.bfloat16)
    block_rows = proto_weight.shape[0] // 16
    width = proto_weight.shape[1]
    blocks = proto_unit.reshape(16, block_rows, width)
    crop_count = student_unit.shape[0]

    def teacher_exp(proto_block):
        return jnp.exp(logits_block(teacher_unit, proto_block, teacher_temp))

    def student_sum(running, proto_block):
        return (running + lax.optimization_barrier(jnp.sum(jnp.exp(logits_block(student_unit, proto_block, student_temp)), axis=1)), None)
    stud_total, unused = lax.scan(student_sum, jnp.zeros((crop_count,), jnp.float32), blocks)
    log_total = jnp.log(stud_total)

    def sweep_once(crop_weight):

        def visit_block(running, proto_block):
            exponent = teacher_exp(proto_block)
            column_scale = 1.0 / jnp.dot(crop_weight, exponent, precision=precise)
            return (running + jnp.dot(exponent, column_scale, precision=precise), column_scale)
        running, scales = lax.scan(visit_block, jnp.zeros((crop_count,), jnp.float32), blocks)
        return (1.0 / running, scales)
    crop_weight = jnp.ones((crop_count,), jnp.float32)
    for sweep_index in range(SWEEPS):
        crop_weight, scales = sweep_once(crop_weight)

    def finish(state_pair, inputs_pair):
        loss_part, grad_unit = state_pair
        proto_block, column_scale = inputs_pair
        exponent = teacher_exp(proto_block)
        assign = crop_weight[:, None] * exponent * column_scale[None, :]
        shifted = logits_block(student_unit, proto_block, student_temp) - log_total[:, None]
        gradient = (loss_scale * (jnp.exp(shifted) - assign)).astype(jnp.bfloat16)
        gradient_wide = gradient.astype(jnp.float32)
        grad_unit = grad_unit + jnp.dot(gradient_wide, proto_block.astype(jnp.float32), precision=precise)
        proto_rows = jnp.dot(gradient_wide.T, student_unit.astype(jnp.float32), precision=precise)
        return ((loss_part + jnp.sum(assign * shifted), grad_unit), proto_rows)
    start_state = (jnp.zeros((), jnp.float32), jnp.zeros((crop_count, width), jnp.float32))
    (loss_part, grad_unit), proto_rows = lax.scan(finish, start_state, (blocks, scales))
    grad_student = unit_back(student_feat, grad_unit)
    grad_proto = unit_back(proto_weight, proto_rows.reshape(proto_weight.shape[0], width))
    loss = -loss_part / crop_count
    return (grad_student, grad_proto, loss)
```

```python
import functools
import itertools

import jax
import jax.numpy as jnp
from jax import lax
from jax.experimental import pallas as pl
from jax.experimental.pallas import tpu as pltpu
from jax.sharding import PartitionSpec as P

SWEEPS = 3
X, Y, C = 4, 4, 2
B = 256
D = 256
L = 128
NB = X * C
CR = NB * B
Q = B // Y
LOG2E = 1.4426950408889634
EPS = 1e-6
F32, BF16 = jnp.float32, jnp.bfloat16
MESH = pl.DeviceIdType.MESH
NT = (((1,), (1,)), ((), ()))


def inverse_norm(v):
    return lax.rsqrt(jnp.sum(v * v, axis=1, keepdims=True) + EPS)


def unit_back(v, upstream):
    inv = inverse_norm(v)
    u = v * inv
    return (upstream - u * jnp.sum(u * upstream, axis=1, keepdims=True)) * inv


def ring_distance(d, n):
    return min(d, n - d)


def offsets(sizes):
    every = [o for o in itertools.product(*[range(n) for n in sizes]) if any(o)]
    return sorted(every, key=lambda o: -sum(ring_distance(d, n) for d, n in zip(o, sizes)))


def kernel(Z, sf, tf, pw, gs_o, gp_o, loss_o, T, U, PR, K, S, G, UT, cwb, ltb, part, col, colr, row0, row0r, row, rowr,
           pg, pgr, gu, corer, rsr, gsb, lz, lzr, lx, lxr, cscale, ssem, rsem, csem, xsem):
    H = Z // 2
    dp, y = lax.axis_index("dp"), lax.axis_index("proto")
    z, x, c = dp // (X * C), lax.rem(dp // C, X), lax.rem(dp, C)

    def dev(zz, xx, yy, cc):
        return ((zz * X + xx) * C + cc, yy)

    def at_z(d):
        return dev(lax.rem(z + d, Z), x, y, c)

    def at_xyc(o):
        return dev(z, lax.rem(x + o[0], X), lax.rem(y + o[1], Y), lax.rem(c + o[2], C))

    z_offs = [o[0] for o in offsets((Z,))]
    xyc_offs = offsets((X, Y, C))
    xy_offs = offsets((X, Y))
    partner = at_xyc((0, 0, 1))

    barrier = pltpu.get_barrier_semaphore()
    for d in z_offs:
        pl.semaphore_signal(barrier, 1, device_id=at_z(d), device_id_type=MESH)
    for o in xyc_offs:
        pl.semaphore_signal(barrier, 1, device_id=at_xyc(o), device_id_type=MESH)

    own = x * C + c
    pv = pw[...]
    PR[z] = (pv * inverse_norm(pv)).astype(BF16)
    tv = tf[...].astype(F32)
    T[own] = (tv * inverse_norm(tv)).astype(BF16)
    sv = sf[...].astype(F32)
    U[own] = (sv * inverse_norm(sv)).astype(BF16)
    pl.semaphore_wait(barrier, len(z_offs) + len(xyc_offs))

    count = [0]
    sent = []

    def send(src, dst, device):
        i = count[0]
        count[0] += 1
        copy = pltpu.make_async_remote_copy(src, dst, ssem.at[i], rsem.at[i], device_id=device, device_id_type=MESH)
        copy.start()
        sent.append(copy)
        return copy

    def wait_bytes(ref, sem):
        pltpu.make_async_copy(ref, ref, sem).wait()

    def exchange(src, slots, targets, k):
        for i, device in enumerate(targets):
            pltpu.make_async_remote_copy(
                src, slots.at[i], xsem.at[k], csem.at[k], device_id=device, device_id_type=MESH
            ).start()

    def arrive(slots, k):
        wait_bytes(slots, csem.at[k])

    z_targets = [at_z(d) for d in z_offs]
    xyc_targets = [at_xyc(o) for o in xyc_offs]

    up, down = at_z(1), at_z(Z - 1)
    half = B // 2
    lo, hi = pl.ds(0, half), pl.ds(half, half)
    ring = []
    ring.append([(send(PR.at[z, part_rows], PR.at[z, part_rows], up), send(PR.at[z, part_rows], PR.at[z, part_rows], down))
                 for part_rows in (lo, hi)])

    x_offs = sorted(range(1, X), key=lambda d: -ring_distance(d, X))

    def spread(A):
        return [send(A.at[own], A.at[own], at_xyc((d, 0, 0))) for d in x_offs], [send(A.at[own], A.at[own], partner)]

    def pass_on(A, copies):
        got, to_partner = copies
        for d, copy in zip(x_offs, got):
            copy.wait_recv()
            b = lax.rem(x + X - d, X) * C + c
            to_partner.append(send(A.at[b], A.at[b], partner))

    t_copies = spread(T)
    u_copies = spread(U)
    pass_on(T, t_copies)

    def ring_step(s):
        up_z, down_z = lax.rem(z + Z - s, Z), lax.rem(z + s, Z)
        step = []
        for i, part_rows in enumerate((lo, hi)):
            pair = [None, None]
            if s < H:
                ring[s - 1][i][0].wait_recv()
                ring[s - 1][i][1].wait_recv()
                if s + 1 < H or i == 0:
                    pair[0] = send(PR.at[up_z, part_rows], PR.at[up_z, part_rows], up)
                if s + 1 < H or i == 1:
                    pair[1] = send(PR.at[down_z, part_rows], PR.at[down_z, part_rows], down)
            else:
                ring[s - 1][i][i].wait_recv()
            step.append(pair)
        ring.append(step)

    def teacher_block(zz):
        protos = PR[zz]

        def tile(b, acc):
            logits = lax.dot_general(T[b], protos, NT, preferred_element_type=F32)
            e = jnp.exp2(logits * (25.0 * LOG2E))
            K[zz, pl.ds(pl.multiple_of(b * B, B), B)] = e
            return acc + jnp.sum(e.reshape(B // 8, 8, B), axis=0)

        acc = lax.fori_loop(0, NB, tile, jnp.zeros((8, B), F32))
        col[0, pl.ds(zz, 1)] = jnp.sum(acc, axis=0, keepdims=True)

    for copy in t_copies[1]:
        copy.wait_recv()
    teacher_block(z)
    for s in range(1, H):
        ring_step(s)
        teacher_block(lax.rem(z + Z - s, Z))
        teacher_block(lax.rem(z + s, Z))
        if s == 1:
            pass_on(U, u_copies)
    ring_step(H)
    teacher_block(lax.rem(z + H, Z))
    exchange(col.at[0], colr.at[0], z_targets, 0)

    for copy in u_copies[1]:
        copy.wait_recv()

    def student_tile(b, carry):
        units = U[b]
        rows = pl.ds(pl.multiple_of(b * B, B), B)
        total = jnp.zeros((B, L), F32)
        for zz in range(Z):
            logits = lax.dot_general(units, PR[zz], NT, preferred_element_type=F32)
            S[zz, rows] = logits
            e = jnp.exp2(logits * (10.0 * LOG2E))
            total = total + e[:, :L] + e[:, L:]
        part[rows] = total
        UT[b] = units.T
        return carry

    lax.fori_loop(0, NB, student_tile, 0)
    ones = jnp.ones((8, L), F32)

    def to_lanes(dst, first):
        for b in range(NB):
            sums = lax.dot_general(ones, part[b * B:(b + 1) * B], NT, precision=lax.Precision.HIGHEST, preferred_element_type=F32)
            dst[first + b:first + b + 1, :] = sums[:1]

    def to_rows(dst, values):
        for b in range(NB):
            dst[b * B:(b + 1) * B, :] = jnp.broadcast_to(values[b:b + 1], (L, B)).T

    to_lanes(row0, NB)

    def row_pass(scale):
        wide = [jnp.broadcast_to(scale[zz:zz + 1, h * L:(h + 1) * L], (8, L)) for zz in range(Z) for h in range(2)]

        def tile(r, carry):
            rows = pl.ds(pl.multiple_of(r * 32, 32), 32)
            acc = jnp.zeros((4, 8, L), F32)
            for zz in range(Z):
                for h in range(2):
                    acc = acc + K[zz, rows, h * L:(h + 1) * L].reshape(4, 8, L) * wide[zz * 2 + h][None]
            part[rows] = acc.reshape(32, L)
            return carry

        lax.fori_loop(0, CR // 32, tile, 0)

    def col_pass(k):
        def tile(r, accs):
            rows = pl.ds(pl.multiple_of(r * 32, 32), 32)
            w = cwb[rows].reshape(4, 8, L)
            return tuple(
                accs[zz * 2 + h] + jnp.sum(K[zz, rows, h * L:(h + 1) * L].reshape(4, 8, L) * w, axis=0)
                for zz in range(Z)
                for h in range(2)
            )

        accs = lax.fori_loop(0, CR // 32, tile, (jnp.zeros((8, L), F32),) * (2 * Z))
        for zz in range(Z):
            for h in range(2):
                col[k, zz:zz + 1, h * L:(h + 1) * L] = jnp.sum(accs[zz * 2 + h], axis=0, keepdims=True)

    for k in range(SWEEPS):
        if k > 0:
            col_pass(k)
            exchange(col.at[k], colr.at[k], z_targets, k)
        arrive(colr.at[k], k)
        total = col[k]
        for i in range(len(z_offs)):
            total = total + colr[k, i]
        scale = 1.0 / total
        row_pass(scale)
        mine, slots = (row0, row0r) if k == 0 else (row.at[k - 1], rowr.at[k - 1])
        to_lanes(mine, 0)
        exchange(mine, slots, xyc_targets, SWEEPS + k)
        arrive(slots, SWEEPS + k)
        total = mine[...]
        for i in range(len(xyc_offs)):
            total = total + slots[i]
        to_rows(cwb, 1.0 / total[:NB])
        if k == 0:
            to_rows(ltb, jnp.log(total[NB:]))

    cscale[...] = scale

    def gradient_block(zz, loss):
        cs = cscale[pl.ds(zz, 1)]

        def tile(b, loss):
            rows = pl.ds(pl.multiple_of(b * B, B), B)
            w, lt = cwb[rows], ltb[rows]
            w = jnp.concatenate([w, w], axis=1)
            lt = jnp.concatenate([lt, lt], axis=1)
            assign = K[zz, rows] * w * cs
            shifted = S[zz, rows] * 10.0 - lt
            e = jnp.exp2(shifted * LOG2E)
            G[zz, rows] = ((e - assign) * 1024.0).astype(BF16)
            return loss + jnp.sum((assign * shifted).reshape(B // 8, 8, B), axis=0)

        loss = lax.fori_loop(0, NB, tile, loss)

        def contract(b, carry):
            pg[zz] += jnp.dot(UT[b], G[zz, pl.ds(pl.multiple_of(b * B, B), B)], preferred_element_type=F32)
            return carry

        pg[zz] = jnp.zeros((D, B), F32)
        lax.fori_loop(0, NB, contract, 0)
        return loss

    def zi(d):
        return lax.rem(z + d, Z)

    steps = []

    def reduce_step(s):
        if s > 1:
            d = H - s + 1
            for way, zz in ((0, zi(d)), (1, zi(Z - d))):
                steps[-1][way].wait_recv()
                if s == 2:
                    rows = (lo, hi)[way]
                    pg[zz, rows] += pgr[way, 0, rows]
                else:
                    pg[zz] += pgr[way, s - 2]
        if s <= H:
            d = H - s + 1
            if s == 1:
                steps.append((send(pg.at[zi(H), lo], pgr.at[0, 0, lo], up), send(pg.at[zi(H), hi], pgr.at[1, 0, hi], down)))
            else:
                steps.append((send(pg.at[zi(d)], pgr.at[0, s - 1], up), send(pg.at[zi(Z - d)], pgr.at[1, s - 1], down)))

    loss = gradient_block(zi(H), jnp.zeros((8, B), F32))
    reduce_step(1)
    for d in range(H - 1, 0, -1):
        loss = gradient_block(zi(d), loss)
        loss = gradient_block(zi(Z - d), loss)
        if d == max(H - 2, 1):
            reduce_step(2)
    loss = gradient_block(z, loss)

    lz[...] = loss[:, :L] + loss[:, L:]
    exchange(lz, lzr, z_targets, 2 * SWEEPS)

    def crop_block(b):
        acc = jnp.dot(G[0, pl.ds(pl.multiple_of(b * B, B), B)], PR[0], preferred_element_type=F32)
        for zz in range(1, Z):
            acc = acc + jnp.dot(G[zz, pl.ds(pl.multiple_of(b * B, B), B)], PR[zz], preferred_element_type=F32)
        gu[b] = acc

    x_order = [*x_offs, 0]
    core_copies = []
    for d in x_order:
        b = lax.rem(x + d, X) * C + (1 - c)
        crop_block(b)
        core_copies.append(send(gu.at[b], corer.at[lax.rem(x + d, X)], partner))
    reduce_step(3)
    scattered = []
    for d, copy in zip(x_order, core_copies):
        xx = lax.rem(x + d, X)
        b = xx * C + c
        crop_block(b)
        copy.wait_recv()
        gu[b] += corer[xx]
        for i, (ox, oy) in enumerate(xy_offs):
            if ox == d:
                q = pl.ds(pl.multiple_of(lax.rem(y + oy, Y) * Q, Q), Q)
                scattered.append(send(gu.at[b, q], rsr.at[i], at_xyc((ox, oy, 0))))
    arrive(lzr, 2 * SWEEPS)
    total = lz[...]
    for i in range(len(z_offs)):
        total = total + lzr[i]
    lx[...] = total
    exchange(lx, lxr, xyc_targets, 2 * SWEEPS + 1)
    reduce_step(4)
    for copy in scattered:
        copy.wait_recv()
    mine = pl.ds(pl.multiple_of(y * Q, Q), Q)
    total = gu[own, mine]
    for i in range(len(xy_offs)):
        total = total + rsr[i]
    gsb[mine] = unit_back(sf[mine].astype(F32), total)
    y_copies = [send(gsb.at[mine], gsb.at[mine], at_xyc((0, d, 0))) for d in sorted(range(1, Y), key=lambda d: -ring_distance(d, Y))]

    arrive(lxr, 2 * SWEEPS + 1)
    total = lx[...]
    for i in range(len(xyc_offs)):
        total = total + lxr[i]
    loss_o[...] = total

    for way in range(2):
        steps[-1][way].wait_recv()
    rows_sum = (pg[z] + pgr[0, H - 1] + pgr[1, H - 1]).T
    gp_o[...] = unit_back(pw[...], rows_sum)
    for copy in y_copies:
        copy.wait_recv()
    gs_o[...] = gsb[...]

    for copy in sent:
        copy.wait_send()
    for k in range(SWEEPS):
        wait_bytes(colr.at[k], xsem.at[k])
    wait_bytes(row0r, xsem.at[SWEEPS])
    for k in range(1, SWEEPS):
        wait_bytes(rowr.at[k - 1], xsem.at[SWEEPS + k])
    wait_bytes(lzr, xsem.at[2 * SWEEPS])
    wait_bytes(lxr, xsem.at[2 * SWEEPS + 1])


def shards(Z, student_feat, teacher_feat, proto_weight):
    H = Z // 2
    nx, nz = X * Y * C - 1, Z - 1
    vmem = pl.BlockSpec(memory_space=pltpu.VMEM)
    v = pltpu.VMEM
    copies = 256
    gs, gp, loss = pl.pallas_call(
        functools.partial(kernel, Z),
        out_shape=(
            jax.ShapeDtypeStruct((B, D), F32),
            jax.ShapeDtypeStruct((B, D), F32),
            jax.ShapeDtypeStruct((8, L), F32),
        ),
        in_specs=[vmem] * 3,
        out_specs=(vmem,) * 3,
        scratch_shapes=[
            v((NB, B, D), BF16), v((NB, B, D), BF16), v((Z, B, D), BF16),
            v((Z, CR, B), F32), v((Z, CR, B), F32), v((Z, CR, B), BF16), v((NB, D, B), BF16),
            v((CR, L), F32), v((CR, L), F32), v((CR, L), F32),
            v((SWEEPS, Z, B), F32), v((SWEEPS, nz, Z, B), F32),
            v((2 * NB, B), F32), v((nx, 2 * NB, B), F32),
            v((SWEEPS - 1, NB, B), F32), v((SWEEPS - 1, nx, NB, B), F32),
            v((Z, D, B), F32), v((2, H, D, B), F32), v((NB, B, D), F32), v((X, B, D), F32),
            v((X * Y - 1, Q, D), F32), v((B, D), F32),
            v((8, L), F32), v((nz, 8, L), F32), v((8, L), F32), v((nx, 8, L), F32), v((Z, B), F32),
            pltpu.SemaphoreType.DMA((copies,)), pltpu.SemaphoreType.DMA((copies,)),
            pltpu.SemaphoreType.DMA((2 * SWEEPS + 2,)), pltpu.SemaphoreType.DMA((2 * SWEEPS + 2,)),
        ],
        compiler_params=pltpu.CompilerParams(
            collective_id=0, has_side_effects=True, vmem_limit_bytes=62 * 2**20
        ),
        cost_estimate=pl.CostEstimate(flops=8 * CR * Z * B * D, bytes_accessed=2**21, transcendentals=2 * CR * Z * B),
    )(student_feat, teacher_feat, proto_weight)
    crops = NB * Z * B
    return gs, gp, -jnp.sum(loss) / crops


def solution(mesh):
    Z = mesh.shape["dp"] // (X * C)
    return jax.shard_map(
        functools.partial(shards, Z),
        mesh=mesh,
        in_specs=(P("dp", None), P("dp", None), P(("proto", "dp"), None)),
        out_specs=(P("dp", None), P(("proto", "dp"), None), P()),
        check_vma=False,
    )
```

```python
import functools
import itertools

import jax
import jax.numpy as jnp
from jax import lax
from jax.experimental import pallas as pl
from jax.experimental.pallas import tpu as pltpu
from jax.sharding import PartitionSpec as P

SWEEPS = 3
X, Y, C = 4, 4, 2
B = 256
D = 256
L = 128
NB = X * C
CR = NB * B
Q = B // Y
NP = 4
SCALE = 1024.0
LOG2E = 1.4426950408889634
EPS = 1e-6
F32, BF16 = jnp.float32, jnp.bfloat16
MESH = pl.DeviceIdType.MESH
NT = (((1,), (1,)), ((), ()))


def inverse_norm(v):
    return lax.rsqrt(jnp.sum(v * v, axis=1, keepdims=True) + EPS)


def unit_back(v, upstream):
    inv = inverse_norm(v)
    u = v * inv
    return (upstream - u * jnp.sum(u * upstream, axis=1, keepdims=True)) * inv


def ring_distance(d, n):
    return min(d, n - d)


def offsets(sizes):
    every = [o for o in itertools.product(*[range(n) for n in sizes]) if any(o)]
    return sorted(every, key=lambda o: -sum(ring_distance(d, n) for d, n in zip(o, sizes)))


def kernel(Z, sf, tf, pw, gs_o, gp_o, loss_o, T, U, PR, K, S, G, cwb, ltb, part, col, colr, stud, studr, row, rowr,
           pg, near, nearr, nxt, nxtr, pgr, corer, rss, rsr, gsb, lz, lzr, lx, lxr, cscale, ssem, rsem, csem, xsem):
    H = Z // 2
    dp, y = lax.axis_index("dp"), lax.axis_index("proto")
    z, x, c = dp // (X * C), lax.rem(dp // C, X), lax.rem(dp, C)

    def dev(zz, xx, yy, cc):
        return ((zz * X + xx) * C + cc, yy)

    def at_z(d):
        return dev(lax.rem(z + d, Z), x, y, c)

    def at_xyc(o):
        return dev(z, lax.rem(x + o[0], X), lax.rem(y + o[1], Y), lax.rem(c + o[2], C))

    z_offs = [o[0] for o in offsets((Z,))]
    xyc_offs = offsets((X, Y, C))
    xy_offs = offsets((X, Y))
    partner = at_xyc((0, 0, 1))

    barrier = pltpu.get_barrier_semaphore()
    for d in z_offs:
        pl.semaphore_signal(barrier, 1, device_id=at_z(d), device_id_type=MESH)
    for o in xyc_offs:
        pl.semaphore_signal(barrier, 1, device_id=at_xyc(o), device_id_type=MESH)

    own = x * C + c
    pv = pw[...]
    PR[z] = (pv * inverse_norm(pv)).astype(BF16)
    tv = tf[...].astype(F32)
    T[own] = (tv * inverse_norm(tv)).astype(BF16)
    sv = sf[...].astype(F32)
    U[own] = (sv * inverse_norm(sv)).astype(BF16)
    pl.semaphore_wait(barrier, len(z_offs) + len(xyc_offs))

    count = [0]
    sent = []

    def send(src, dst, device):
        i = count[0]
        count[0] += 1
        copy = pltpu.make_async_remote_copy(src, dst, ssem.at[i], rsem.at[i], device_id=device, device_id_type=MESH)
        copy.start()
        sent.append(copy)
        return copy

    def wait_bytes(ref, sem):
        pltpu.make_async_copy(ref, ref, sem).wait()

    def exchange(src, slots, targets, k):
        for i, device in enumerate(targets):
            pltpu.make_async_remote_copy(
                src, slots.at[i], xsem.at[k], csem.at[k], device_id=device, device_id_type=MESH
            ).start()

    def arrive(slots, k):
        wait_bytes(slots, csem.at[k])

    z_targets = [at_z(d) for d in z_offs]
    xyc_targets = [at_xyc(o) for o in xyc_offs]

    up, down = at_z(1), at_z(Z - 1)
    half = B // 2
    lo, hi = pl.ds(0, half), pl.ds(half, half)
    pieces = [pl.ds(i * (B // NP), B // NP) for i in range(NP)]
    ring = [[[send(PR.at[z, rows], PR.at[z, rows], way) for rows in pieces] for way in (up, down)]]

    x_offs = sorted(range(1, X), key=lambda d: -ring_distance(d, X))

    def spread(A):
        return [send(A.at[own], A.at[own], at_xyc((d, 0, 0))) for d in x_offs], [send(A.at[own], A.at[own], partner)]

    def pass_on(A, copies):
        got, to_partner = copies
        for d, copy in zip(x_offs, got):
            copy.wait_recv()
            b = lax.rem(x + X - d, X) * C + c
            to_partner.append(send(A.at[b], A.at[b], partner))

    t_copies = spread(T)

    def ring_step(s):
        step = [[None] * NP, [None] * NP]
        for i, rows in enumerate(pieces):
            for w, (zz, way) in enumerate(((lax.rem(z + Z - s, Z), up), (lax.rem(z + s, Z), down))):
                if ring[s - 1][w][i] is not None:
                    ring[s - 1][w][i].wait_recv()
                    if s + 1 < H or (s < H and (i < NP // 2) == (w == 0)):
                        step[w][i] = send(PR.at[zz, rows], PR.at[zz, rows], way)
        ring.append(step)

    def teacher_block(zz):
        protos = PR[zz]

        def tile(b, acc):
            logits = lax.dot_general(T[b], protos, NT, preferred_element_type=F32)
            e = jnp.exp2(logits * (25.0 * LOG2E))
            K[zz, pl.ds(pl.multiple_of(b * B, B), B)] = e
            return acc + jnp.sum(e.reshape(B // 8, 8, B), axis=0)

        acc = lax.fori_loop(0, NB, tile, jnp.zeros((8, B), F32), unroll=NB)
        col[0, pl.ds(zz, 1)] = jnp.sum(acc, axis=0, keepdims=True)

    ring_step(1)
    pass_on(T, t_copies)
    u_copies = spread(U)
    for s in range(2, H):
        ring_step(s)
        if s == 2:
            for copy in t_copies[1]:
                copy.wait_recv()
            teacher_block(z)
        else:
            pass_on(U, u_copies)
        teacher_block(lax.rem(z + Z - s + 1, Z))
        teacher_block(lax.rem(z + s - 1, Z))
    ring_step(H)
    teacher_block(lax.rem(z + Z - H + 1, Z))
    teacher_block(lax.rem(z + H - 1, Z))
    teacher_block(lax.rem(z + H, Z))
    exchange(col.at[0], colr.at[0], z_targets, 0)

    for copy in u_copies[1]:
        copy.wait_recv()

    part[...] = jnp.zeros_like(part)

    def student_block(zz, carry):
        protos = PR[zz]

        def tile(b, carry):
            rows = pl.ds(pl.multiple_of(b * B, B), B)
            scores = lax.dot_general(U[b], protos, NT, preferred_element_type=F32) * (10.0 * LOG2E)
            S[zz, rows] = scores
            e = jnp.exp2(scores)
            part[rows] += e[:, :L] + e[:, L:]
            return carry

        return lax.fori_loop(0, NB, tile, carry, unroll=NB)

    lax.fori_loop(0, Z, student_block, 0)
    used = t_copies[0] + t_copies[1]
    for copy in used:
        copy.wait_send()
    sent[:] = [copy for copy in sent if all(copy is not other for other in used)]
    UT = T
    for b in range(NB):
        UT[b] = U[b].T

    def to_lanes(dst):
        for b in range(NB):
            dst[b:b + 1, :] = jnp.sum(part[b * B:(b + 1) * B].T, axis=0, keepdims=True)

    def to_rows(dst, values):
        for b in range(NB):
            dst[b * B:(b + 1) * B, :] = jnp.broadcast_to(values[b:b + 1], (L, B)).T

    to_lanes(stud)

    R = 128

    def row_pass(scale):
        wide = [jnp.broadcast_to(scale[zz:zz + 1, h * L:(h + 1) * L], (8, L)) for zz in range(Z) for h in range(2)]

        def tile(r, carry):
            rows = pl.ds(pl.multiple_of(r * R, R), R)
            acc = jnp.zeros((R // 8, 8, L), F32)
            for zz in range(Z):
                for h in range(2):
                    acc = acc + K[zz, rows, h * L:(h + 1) * L].reshape(R // 8, 8, L) * wide[zz * 2 + h][None]
            part[rows] = acc.reshape(R, L)
            return carry

        lax.fori_loop(0, CR // R, tile, 0, unroll=2)

    def col_pass(k):
        def tile(r, accs):
            rows = pl.ds(pl.multiple_of(r * R, R), R)
            w = cwb[rows].reshape(R // 8, 8, L)
            return tuple(
                accs[zz * 2 + h] + jnp.sum(K[zz, rows, h * L:(h + 1) * L].reshape(R // 8, 8, L) * w, axis=0)
                for zz in range(Z)
                for h in range(2)
            )

        accs = lax.fori_loop(0, CR // R, tile, (jnp.zeros((8, L), F32),) * (2 * Z), unroll=2)
        for zz in range(Z):
            for h in range(2):
                col[k, zz:zz + 1, h * L:(h + 1) * L] = jnp.sum(accs[zz * 2 + h], axis=0, keepdims=True)

    for k in range(SWEEPS):
        if k > 0:
            col_pass(k)
            exchange(col.at[k], colr.at[k], z_targets, k)
        arrive(colr.at[k], k)
        total = col[k]
        for i in range(len(z_offs)):
            total = total + colr[k, i]
        scale = 1.0 / total
        row_pass(scale)
        mine, slots = row.at[k], rowr.at[k]
        to_lanes(mine)
        exchange(mine, slots, xyc_targets, SWEEPS + k)
        if k == 0:
            exchange(stud, studr, xyc_targets, 2 * SWEEPS + 2)
        arrive(slots, SWEEPS + k)
        total = mine[...]
        for i in range(len(xyc_offs)):
            total = total + slots[i]
        to_rows(cwb, 1.0 / total)
        if k == 1:
            arrive(studr, 2 * SWEEPS + 2)
            total = stud[...]
            for i in range(len(xyc_offs)):
                total = total + studr[i]
            to_rows(ltb, jnp.log(total) * LOG2E)

    cscale[...] = scale

    def gradient_block(zz, loss):
        cs = cscale[pl.ds(zz, 1)]

        acc = jnp.zeros((D, B), F32)
        for b in range(NB):
            rows = slice(b * B, (b + 1) * B)
            w, lt = cwb[rows], ltb[rows]
            w = jnp.concatenate([w, w], axis=1)
            lt = jnp.concatenate([lt, lt], axis=1)
            assign = K[zz, rows] * w * cs
            shifted = S[zz, rows] - lt
            g = (jnp.exp2(shifted) - assign).astype(BF16)
            G[zz, rows] = g
            loss = loss + jnp.sum((assign * shifted).reshape(B // 8, 8, B), axis=0)
            acc = acc + jnp.dot(UT[b], g, preferred_element_type=F32)
        pg[zz] = acc
        return loss

    def zi(d):
        return lax.rem(z + d, Z)

    steps = []

    def reduce_step(s):
        d = H - s + 1
        step = [[], []]
        for i, rows in enumerate((lo, hi)):
            for w, (zz, way) in enumerate(((zi(d), up), (zi(Z - d), down))):
                if s == 1:
                    if i == w:
                        near[w, rows] = pg[zz, rows].astype(BF16)
                        step[w].append(send(near.at[w, rows], nearr.at[w, rows], way))
                elif s == 2:
                    total = pg[zz, rows]
                    if i == w:
                        steps[-1][w][0].wait_recv()
                        total = total + nearr[w, rows].astype(F32)
                    nxt[w, rows] = total.astype(BF16)
                    step[w].append(send(nxt.at[w, rows], nxtr.at[w, rows], way))
                else:
                    steps[-1][w][i].wait_recv()
                    came = nxtr[w, rows].astype(F32) if s == 3 else pgr[w, s - 4, rows]
                    pg[zz, rows] += came
                    if s <= H:
                        step[w].append(send(pg.at[zz, rows], pgr.at[w, s - 3, rows], way))
        steps.append(step)

    loss = gradient_block(zi(H), jnp.zeros((8, B), F32))
    reduce_step(1)
    for d in range(H - 1, 0, -1):
        loss = gradient_block(zi(d), loss)
        loss = gradient_block(zi(Z - d), loss)
        if d == H - 2:
            reduce_step(2)
    loss = gradient_block(z, loss)

    lz[...] = loss[:, :L] + loss[:, L:]
    exchange(lz, lzr, z_targets, 2 * SWEEPS)

    def gu(b, first=0, n=B):
        return K.at[0, pl.ds(pl.multiple_of(b * B + first, n), n)]

    def crop_block(b):
        acc = jnp.dot(G[0, pl.ds(pl.multiple_of(b * B, B), B)], PR[0], preferred_element_type=F32)
        for zz in range(1, Z):
            acc = acc + jnp.dot(G[zz, pl.ds(pl.multiple_of(b * B, B), B)], PR[zz], preferred_element_type=F32)
        gu(b)[...] = acc

    x_order = [*x_offs, 0]
    core_copies = []
    for d in x_order:
        b = lax.rem(x + d, X) * C + (1 - c)
        crop_block(b)
        core_copies.append(send(gu(b), corer.at[lax.rem(x + d, X)], partner))
    reduce_step(3)
    scattered = []
    for d, copy in zip(x_order, core_copies):
        xx = lax.rem(x + d, X)
        b = xx * C + c
        crop_block(b)
        copy.wait_recv()
        total = gu(b)[...] + corer[xx]
        gu(b)[...] = total
        rss[xx] = total.astype(BF16)
        for i, (ox, oy) in enumerate(xy_offs):
            if ox == d:
                q = pl.ds(pl.multiple_of(lax.rem(y + oy, Y) * Q, Q), Q)
                scattered.append(send(rss.at[xx, q], rsr.at[i], at_xyc((ox, oy, 0))))
    arrive(lzr, 2 * SWEEPS)
    total = lz[...]
    for i in range(len(z_offs)):
        total = total + lzr[i]
    lx[...] = total
    exchange(lx, lxr, xyc_targets, 2 * SWEEPS + 1)
    reduce_step(4)
    for copy in scattered:
        copy.wait_recv()
    mine = pl.ds(pl.multiple_of(y * Q, Q), Q)
    total = gu(own, y * Q, Q)[...]
    for i in range(len(xy_offs)):
        total = total + rsr[i].astype(F32)
    gsb[mine] = total
    y_copies = [send(gsb.at[mine], gsb.at[mine], at_xyc((0, d, 0))) for d in sorted(range(1, Y), key=lambda d: -ring_distance(d, Y))]

    arrive(lxr, 2 * SWEEPS + 1)
    total = lx[...]
    for i in range(len(xyc_offs)):
        total = total + lxr[i]
    loss_o[...] = total

    reduce_step(H + 1)
    gp_o[...] = pg[z].T
    for copy in y_copies:
        copy.wait_recv()
    gs_o[...] = gsb[...]

    for copy in sent:
        copy.wait_send()
    for k in range(SWEEPS):
        wait_bytes(colr.at[k], xsem.at[k])
        wait_bytes(rowr.at[k], xsem.at[SWEEPS + k])
    wait_bytes(studr, xsem.at[2 * SWEEPS + 2])
    wait_bytes(lzr, xsem.at[2 * SWEEPS])
    wait_bytes(lxr, xsem.at[2 * SWEEPS + 1])


def finish(crops, sf, pw, gs, gp, loss, gs_o, gp_o, loss_o):
    gs_o[...] = unit_back(sf[...].astype(F32), gs[...] * SCALE)
    gp_o[...] = unit_back(pw[...], gp[...] * SCALE)
    loss_o[0, 0] = jnp.sum(loss[...]) * (-1.0 / (LOG2E * crops))


def shards(Z, student_feat, teacher_feat, proto_weight):
    H = Z // 2
    nx, nz = X * Y * C - 1, Z - 1
    vmem = pl.BlockSpec(memory_space=pltpu.VMEM)
    v = pltpu.VMEM
    copies = 256
    gs, gp, loss = pl.pallas_call(
        functools.partial(kernel, Z),
        out_shape=(
            jax.ShapeDtypeStruct((B, D), F32),
            jax.ShapeDtypeStruct((B, D), F32),
            jax.ShapeDtypeStruct((8, L), F32),
        ),
        in_specs=[vmem] * 3,
        out_specs=(vmem,) * 3,
        scratch_shapes=[
            v((NB, B, D), BF16), v((NB, B, D), BF16), v((Z, B, D), BF16),
            v((Z, CR, B), F32), v((Z, CR, B), F32), v((Z, CR, B), BF16),
            v((CR, L), F32), v((CR, L), F32), v((CR, L), F32),
            v((SWEEPS, Z, B), F32), v((SWEEPS, nz, Z, B), F32),
            v((NB, B), F32), v((nx, NB, B), F32),
            v((SWEEPS, NB, B), F32), v((SWEEPS, nx, NB, B), F32),
            v((Z, D, B), F32), v((2, D, B), BF16), v((2, D, B), BF16), v((2, D, B), BF16), v((2, D, B), BF16),
            v((2, H - 2, D, B), F32), v((X, B, D), F32), v((X, B, D), BF16),
            v((X * Y - 1, Q, D), BF16), v((B, D), F32),
            v((8, L), F32), v((nz, 8, L), F32), v((8, L), F32), v((nx, 8, L), F32), v((Z, B), F32),
            pltpu.SemaphoreType.DMA((copies,)), pltpu.SemaphoreType.DMA((copies,)),
            pltpu.SemaphoreType.DMA((2 * SWEEPS + 3,)), pltpu.SemaphoreType.DMA((2 * SWEEPS + 3,)),
        ],
        compiler_params=pltpu.CompilerParams(
            collective_id=0, has_side_effects=True, vmem_limit_bytes=62 * 2**20
        ),
        cost_estimate=pl.CostEstimate(flops=8 * CR * Z * B * D, bytes_accessed=2**21, transcendentals=2 * CR * Z * B),
    )(student_feat, teacher_feat, proto_weight)
    gs, gp, loss = pl.pallas_call(
        functools.partial(finish, NB * Z * B),
        out_shape=(
            jax.ShapeDtypeStruct((B, D), F32),
            jax.ShapeDtypeStruct((B, D), F32),
            jax.ShapeDtypeStruct((1, 1), F32),
        ),
        in_specs=[vmem] * 5,
        out_specs=(vmem, vmem, pl.BlockSpec(memory_space=pltpu.SMEM)),
    )(student_feat, proto_weight, gs, gp, loss)
    return gs, gp, loss.reshape(())


def solution(mesh):
    Z = mesh.shape["dp"] // (X * C)
    return jax.shard_map(
        functools.partial(shards, Z),
        mesh=mesh,
        in_specs=(P("dp", None), P("dp", None), P(("proto", "dp"), None)),
        out_specs=(P("dp", None), P(("proto", "dp"), None), P()),
        check_vma=False,
    )
```

```python
import functools
import itertools

import jax
import jax.numpy as jnp
from jax import lax
from jax.experimental import pallas as pl
from jax.experimental.pallas import tpu as pltpu
from jax.sharding import PartitionSpec as P

SWEEPS = 3
X, Y, C = 4, 4, 2
B = 256
D = 256
L = 128
NB = X * C
CR = NB * B
Q = B // Y
NP = 4
SCALE = 1024.0
LOG2E = 1.4426950408889634
EPS = 1e-6
F32, BF16 = jnp.float32, jnp.bfloat16
MESH = pl.DeviceIdType.MESH
NT = (((1,), (1,)), ((), ()))


def inverse_norm(v):
    return lax.rsqrt(jnp.sum(v * v, axis=1, keepdims=True) + EPS)


def unit_back(v, upstream):
    inv = inverse_norm(v)
    u = v * inv
    return (upstream - u * jnp.sum(u * upstream, axis=1, keepdims=True)) * inv


def ring_distance(d, n):
    return min(d, n - d)


def offsets(sizes):
    every = [o for o in itertools.product(*[range(n) for n in sizes]) if any(o)]
    return sorted(every, key=lambda o: -sum(ring_distance(d, n) for d, n in zip(o, sizes)))


def kernel(Z, sf_in, tf_in, pw_in, gs_o, gp_o, loss_o, T, U, PR, K, S, G, cwb, ltb, part, col, colr, stud, studr, wide_row, row, rowr,
           pg, near, nearr, nxt, nxtr, pgr, corer, rss, rsr, gsb, lz, lzr, lx, lxr, cscale, sf, tf, pw, lsem, ssem, rsem, csem, xsem):
    H = ZH = Z // 2
    dp, y = lax.axis_index("dp"), lax.axis_index("proto")
    z, x, c = dp // (X * C), lax.rem(dp // C, X), lax.rem(dp, C)

    def dev(zz, xx, yy, cc):
        return ((zz * X + xx) * C + cc, yy)

    def at_z(d):
        return dev(lax.rem(z + d, Z), x, y, c)

    def at_xyc(o):
        return dev(z, lax.rem(x + o[0], X), lax.rem(y + o[1], Y), lax.rem(c + o[2], C))

    z_offs = [o[0] for o in offsets((Z,))]
    xyc_offs = offsets((X, Y, C))
    xy_offs = offsets((X, Y))
    partner = at_xyc((0, 0, 1))

    loads = [
        pltpu.make_async_copy(src, dst, lsem.at[i]) for i, (src, dst) in enumerate(((pw_in, pw), (tf_in, tf), (sf_in, sf)))
    ]
    for load in loads:
        load.start()
    barrier = pltpu.get_barrier_semaphore()
    for d in z_offs:
        pl.semaphore_signal(barrier, 1, device_id=at_z(d), device_id_type=MESH)
    for o in xyc_offs:
        pl.semaphore_signal(barrier, 1, device_id=at_xyc(o), device_id_type=MESH)

    own = x * C + c

    def unit_into(dst, load, src):
        load.wait()
        v = src[...].astype(F32)
        dst[...] = (v * inverse_norm(v)).astype(BF16)

    unit_into(PR.at[z], loads[0], pw)
    pl.semaphore_wait(barrier, len(z_offs) + len(xyc_offs))

    count = [0]
    sent = []

    def send(src, dst, device):
        i = count[0]
        count[0] += 1
        copy = pltpu.make_async_remote_copy(src, dst, ssem.at[i], rsem.at[i], device_id=device, device_id_type=MESH)
        copy.start()
        sent.append(copy)
        return copy

    def wait_bytes(ref, sem):
        pltpu.make_async_copy(ref, ref, sem).wait()

    def exchange(src, slots, targets, k):
        for i, device in enumerate(targets):
            pltpu.make_async_remote_copy(
                src, slots.at[i], xsem.at[k], csem.at[k], device_id=device, device_id_type=MESH
            ).start()

    def arrive(slots, k):
        wait_bytes(slots, csem.at[k])

    z_targets = [at_z(d) for d in z_offs]
    xyc_targets = [at_xyc(o) for o in xyc_offs]

    up, down = at_z(1), at_z(Z - 1)
    half = B // 2
    lo, hi = pl.ds(0, half), pl.ds(half, half)
    pieces = [pl.ds(i * (B // NP), B // NP) for i in range(NP)]
    ring = [[[send(PR.at[z, rows], PR.at[z, rows], way) for rows in pieces] for way in (up, down)]]

    x_offs = sorted(range(1, X), key=lambda d: -ring_distance(d, X))

    def spread(A):
        return [send(A.at[own], A.at[own], at_xyc((d, 0, 0))) for d in x_offs], [send(A.at[own], A.at[own], partner)]

    def pass_on(A, copies):
        got, to_partner = copies
        for d, copy in zip(x_offs, got):
            copy.wait_recv()
            b = lax.rem(x + X - d, X) * C + c
            to_partner.append(send(A.at[b], A.at[b], partner))

    unit_into(T.at[own], loads[1], tf)
    t_copies = spread(T)
    unit_into(U.at[own], loads[2], sf)

    def ring_step(s):
        step = [[None] * NP, [None] * NP]
        for i, rows in enumerate(pieces):
            for w, (zz, way) in enumerate(((lax.rem(z + Z - s, Z), up), (lax.rem(z + s, Z), down))):
                if ring[s - 1][w][i] is not None:
                    ring[s - 1][w][i].wait_recv()
                    if s + 1 < H or (s < H and (i < NP // 2) == (w == 0)):
                        step[w][i] = send(PR.at[zz, rows], PR.at[zz, rows], way)
        ring.append(step)

    def teacher_block(zz):
        protos = PR[zz]

        def tile(b, acc):
            logits = lax.dot_general(T[b], protos, NT, preferred_element_type=F32)
            e = jnp.exp2(logits * (25.0 * LOG2E))
            K[zz, pl.ds(pl.multiple_of(b * B, B), B)] = e
            return acc + jnp.sum(e.reshape(B // 8, 8, B), axis=0)

        acc = lax.fori_loop(0, NB, tile, jnp.zeros((8, B), F32), unroll=NB)
        sums = jnp.sum(acc, axis=0, keepdims=True)
        for h in range(2):
            col[0, zz // ZH, pl.ds(lax.rem(zz, ZH) * 2 + h, 1)] = sums[:, h * L:(h + 1) * L]

    ring_step(1)
    pass_on(T, t_copies)
    u_copies = spread(U)
    for s in range(2, H):
        ring_step(s)
        if s == 2:
            for copy in t_copies[1]:
                copy.wait_recv()
            teacher_block(z)
        else:
            pass_on(U, u_copies)
        teacher_block(lax.rem(z + Z - s + 1, Z))
        teacher_block(lax.rem(z + s - 1, Z))
    ring_step(H)
    teacher_block(lax.rem(z + Z - H + 1, Z))
    teacher_block(lax.rem(z + H - 1, Z))
    teacher_block(lax.rem(z + H, Z))
    def col_exchange(k, part_of):
        exchange(col.at[k, part_of], colr.at[k, part_of], z_targets, k + part_of * (2 * SWEEPS + 3))

    col_exchange(0, 0)
    col_exchange(0, 1)

    for copy in u_copies[1]:
        copy.wait_recv()

    part[...] = jnp.zeros_like(part)

    def student_block(zz, carry):
        protos = PR[zz]

        def tile(b, carry):
            rows = pl.ds(pl.multiple_of(b * B, B), B)
            scores = lax.dot_general(U[b], protos, NT, preferred_element_type=F32) * (10.0 * LOG2E)
            S[zz, rows] = scores
            e = jnp.exp2(scores)
            part[rows] += e[:, :L] + e[:, L:]
            return carry

        return lax.fori_loop(0, NB, tile, carry, unroll=NB)

    lax.fori_loop(0, Z, student_block, 0)
    used = t_copies[0] + t_copies[1]
    for copy in used:
        copy.wait_send()
    sent[:] = [copy for copy in sent if all(copy is not other for other in used)]
    UT = T
    for b in range(NB):
        UT[b] = U[b].T

    def to_lanes(dst):
        for b in range(NB):
            sums = jnp.sum(part[b * B:(b + 1) * B].T, axis=0, keepdims=True)
            for h in range(2):
                wide_row[h * NB + b:h * NB + b + 1, :] = sums[:, h * L:(h + 1) * L]
        dst[...] = wide_row[...].astype(BF16)

    def to_rows(dst, values):
        for b in range(NB):
            for h in range(2):
                i = h * NB + b
                dst[b * B + h * L:b * B + (h + 1) * L, :] = jnp.broadcast_to(values[i:i + 1], (L, L)).T

    to_lanes(stud)

    R = 128

    def row_pass(part_of, scale):
        wide = [jnp.broadcast_to(scale[i:i + 1], (8, L)) for i in range(2 * ZH)]

        def tile(r, carry):
            rows = pl.ds(pl.multiple_of(r * R, R), R)
            acc = part[rows].reshape(R // 8, 8, L) if part_of else jnp.zeros((R // 8, 8, L), F32)
            for i in range(2 * ZH):
                zz, h = part_of * ZH + i // 2, i % 2
                acc = acc + K[zz, rows, h * L:(h + 1) * L].reshape(R // 8, 8, L) * wide[i][None]
            part[rows] = acc.reshape(R, L)
            return carry

        lax.fori_loop(0, CR // R, tile, 0, unroll=2)

    def col_pass(k, part_of):
        def tile(r, accs):
            rows = pl.ds(pl.multiple_of(r * R, R), R)
            w = cwb[rows].reshape(R // 8, 8, L)
            return tuple(
                accs[i] + jnp.sum(K[part_of * ZH + i // 2, rows, i % 2 * L:(i % 2 + 1) * L].reshape(R // 8, 8, L) * w, axis=0)
                for i in range(2 * ZH)
            )

        accs = lax.fori_loop(0, CR // R, tile, (jnp.zeros((8, L), F32),) * (2 * ZH), unroll=2)
        for i in range(2 * ZH):
            col[k, part_of, i:i + 1] = jnp.sum(accs[i], axis=0, keepdims=True)

    def prepare():
        def tile(b, carry):
            rows = pl.ds(pl.multiple_of(b * B, B), B)
            lt = jnp.concatenate([ltb[rows], ltb[rows]], axis=1)
            acc = jnp.zeros((B, L), F32)
            for zz in range(Z):
                shifted = S[zz, rows] - lt
                S[zz, rows] = jnp.exp2(shifted)
                weighed = K[zz, rows] * cscale[zz:zz + 1] * shifted
                acc = acc + weighed[:, :L] + weighed[:, L:]
            part[rows] = acc
            return carry

        lax.fori_loop(0, NB, tile, 0)

    for k in range(SWEEPS):
        if k > 0:
            for part_of in range(2):
                col_pass(k, part_of)
                col_exchange(k, part_of)
        for part_of in range(2):
            arrive(colr.at[k, part_of], k + part_of * (2 * SWEEPS + 3))
            total = col[k, part_of]
            for i in range(len(z_offs)):
                total = total + colr[k, part_of, i]
            scale = 1.0 / total
            row_pass(part_of, scale)
            if k == SWEEPS - 1:
                for i in range(2 * ZH):
                    zz, h = part_of * ZH + i // 2, i % 2
                    cscale[zz:zz + 1, h * L:(h + 1) * L] = scale[i:i + 1]
        mine, slots = row.at[k], rowr.at[k]
        to_lanes(mine)
        exchange(mine, slots, xyc_targets, SWEEPS + k)
        if k == 0:
            exchange(stud, studr, xyc_targets, 2 * SWEEPS + 2)
        if k == SWEEPS - 1:
            prepare()
        arrive(slots, SWEEPS + k)
        total = mine[...].astype(F32)
        for i in range(len(xyc_offs)):
            total = total + slots[i].astype(F32)
        to_rows(cwb, 1.0 / total)
        if k == 1:
            arrive(studr, 2 * SWEEPS + 2)
            total = stud[...].astype(F32)
            for i in range(len(xyc_offs)):
                total = total + studr[i].astype(F32)
            to_rows(ltb, jnp.log(total) * LOG2E)


    def gradient_block(zz):
        cs = cscale[pl.ds(zz, 1)]

        acc = jnp.zeros((D, B), F32)
        for b in range(NB):
            rows = slice(b * B, (b + 1) * B)
            w = jnp.concatenate([cwb[rows], cwb[rows]], axis=1)
            g = (S[zz, rows] - K[zz, rows] * w * cs).astype(BF16)
            G[zz, rows] = g
            acc = acc + jnp.dot(UT[b], g, preferred_element_type=F32)
        pg[zz] = acc

    def zi(d):
        return lax.rem(z + d, Z)

    steps = []

    def reduce_step(s, j):
        d = H - s + 1
        if j == 0:
            steps.append([[None, None], [None, None]])
        for w, (zz, way) in enumerate(((zi(d), up), (zi(Z - d), down))):
            i = w if j else 1 - w
            rows = (lo, hi)[i]
            if s == 1:
                if j:
                    near[w, rows] = pg[zz, rows].astype(BF16)
                    steps[-1][w][i] = send(near.at[w, rows], nearr.at[w, rows], way)
            elif s == 2:
                total = pg[zz, rows]
                if j:
                    steps[-2][w][i].wait_recv()
                    total = total + nearr[w, rows].astype(F32)
                nxt[w, rows] = total.astype(BF16)
                steps[-1][w][i] = send(nxt.at[w, rows], nxtr.at[w, rows], way)
            else:
                steps[-2][w][i].wait_recv()
                came = nxtr[w, rows].astype(F32) if s == 3 else pgr[w, s - 4, rows]
                pg[zz, rows] += came
                if s <= H:
                    steps[-1][w][i] = send(pg.at[zz, rows], pgr.at[w, s - 3, rows], way)

    gradient_block(zi(H))
    reduce_step(1, 0)
    reduce_step(1, 1)
    for d in range(H - 1, 0, -1):
        gradient_block(zi(d))
        gradient_block(zi(Z - d))
        if d == H - 1:
            reduce_step(2, 0)
    gradient_block(z)
    reduce_step(2, 1)

    lz[...] = jnp.sum((part[...] * cwb[...]).reshape(CR // 8, 8, L), axis=0)
    exchange(lz, lzr, z_targets, 2 * SWEEPS)

    def gu(b, first=0, n=B):
        return K.at[0, pl.ds(pl.multiple_of(b * B + first, n), n)]

    def crop_block(b):
        acc = jnp.dot(G[0, pl.ds(pl.multiple_of(b * B, B), B)], PR[0], preferred_element_type=F32)
        for zz in range(1, Z):
            acc = acc + jnp.dot(G[zz, pl.ds(pl.multiple_of(b * B, B), B)], PR[zz], preferred_element_type=F32)
        gu(b)[...] = acc

    x_order = [*x_offs, 0]
    core_copies = []
    for d in x_order:
        b = lax.rem(x + d, X) * C + (1 - c)
        crop_block(b)
        core_copies.append(send(gu(b), corer.at[lax.rem(x + d, X)], partner))
    reduce_step(3, 0)
    scattered = []
    for d, copy in zip(x_order, core_copies):
        xx = lax.rem(x + d, X)
        b = xx * C + c
        crop_block(b)
        copy.wait_recv()
        total = gu(b)[...] + corer[xx]
        gu(b)[...] = total
        rss[xx] = total.astype(BF16)
        for i, (ox, oy) in enumerate(xy_offs):
            if ox == d:
                q = pl.ds(pl.multiple_of(lax.rem(y + oy, Y) * Q, Q), Q)
                scattered.append(send(rss.at[xx, q], rsr.at[i], at_xyc((ox, oy, 0))))
    reduce_step(3, 1)
    arrive(lzr, 2 * SWEEPS)
    total = lz[...]
    for i in range(len(z_offs)):
        total = total + lzr[i]
    lx[...] = total
    exchange(lx, lxr, xyc_targets, 2 * SWEEPS + 1)
    reduce_step(4, 0)
    reduce_step(4, 1)
    for copy in scattered:
        copy.wait_recv()
    mine = pl.ds(pl.multiple_of(y * Q, Q), Q)
    total = gu(own, y * Q, Q)[...]
    for i in range(len(xy_offs)):
        total = total + rsr[i].astype(F32)
    gsb[mine] = total
    y_copies = [send(gsb.at[mine], gsb.at[mine], at_xyc((0, d, 0))) for d in sorted(range(1, Y), key=lambda d: -ring_distance(d, Y))]

    arrive(lxr, 2 * SWEEPS + 1)
    total = lx[...]
    for i in range(len(xyc_offs)):
        total = total + lxr[i]
    loss_o[...] = total

    reduce_step(H + 1, 0)
    reduce_step(H + 1, 1)
    gp_o[...] = pg[z].T
    for copy in y_copies:
        copy.wait_recv()
    gs_o[...] = gsb[...]

    for copy in sent:
        copy.wait_send()
    for k in range(SWEEPS):
        for part_of in range(2):
            wait_bytes(colr.at[k, part_of], xsem.at[k + part_of * (2 * SWEEPS + 3)])
        wait_bytes(rowr.at[k], xsem.at[SWEEPS + k])
    wait_bytes(studr, xsem.at[2 * SWEEPS + 2])
    wait_bytes(lzr, xsem.at[2 * SWEEPS])
    wait_bytes(lxr, xsem.at[2 * SWEEPS + 1])


def finish(crops, sf, pw, gs, gp, loss, gs_o, gp_o, loss_o):
    gs_o[...] = unit_back(sf[...].astype(F32), gs[...] * SCALE)
    gp_o[...] = unit_back(pw[...], gp[...] * SCALE)
    loss_o[0, 0] = jnp.sum(loss[...]) * (-1.0 / (LOG2E * crops))


def shards(Z, student_feat, teacher_feat, proto_weight):
    H = Z // 2
    nx, nz = X * Y * C - 1, Z - 1
    vmem = pl.BlockSpec(memory_space=pltpu.VMEM)
    v = pltpu.VMEM
    copies = 256
    gs, gp, loss = pl.pallas_call(
        functools.partial(kernel, Z),
        out_shape=(
            jax.ShapeDtypeStruct((B, D), F32),
            jax.ShapeDtypeStruct((B, D), F32),
            jax.ShapeDtypeStruct((8, L), F32),
        ),
        in_specs=[pl.BlockSpec(memory_space=pl.ANY)] * 3,
        out_specs=(vmem,) * 3,
        scratch_shapes=[
            v((NB, B, D), BF16), v((NB, B, D), BF16), v((Z, B, D), BF16),
            v((Z, CR, B), F32), v((Z, CR, B), F32), v((Z, CR, B), BF16),
            v((CR, L), F32), v((CR, L), F32), v((CR, L), F32),
            v((SWEEPS, 2, Z, L), F32), v((SWEEPS, 2, nz, Z, L), F32),
            v((2 * NB, L), BF16), v((nx, 2 * NB, L), BF16), v((2 * NB, L), F32),
            v((SWEEPS, 2 * NB, L), BF16), v((SWEEPS, nx, 2 * NB, L), BF16),
            v((Z, D, B), F32), v((2, D, B), BF16), v((2, D, B), BF16), v((2, D, B), BF16), v((2, D, B), BF16),
            v((2, H - 2, D, B), F32), v((X, B, D), F32), v((X, B, D), BF16),
            v((X * Y - 1, Q, D), BF16), v((B, D), F32),
            v((8, L), F32), v((nz, 8, L), F32), v((8, L), F32), v((nx, 8, L), F32), v((Z, B), F32),
            v((B, D), BF16), v((B, D), BF16), v((B, D), F32), pltpu.SemaphoreType.DMA((3,)),
            pltpu.SemaphoreType.DMA((copies,)), pltpu.SemaphoreType.DMA((copies,)),
            pltpu.SemaphoreType.DMA((3 * SWEEPS + 3,)), pltpu.SemaphoreType.DMA((3 * SWEEPS + 3,)),
        ],
        compiler_params=pltpu.CompilerParams(
            collective_id=0, has_side_effects=True, vmem_limit_bytes=62 * 2**20
        ),
        cost_estimate=pl.CostEstimate(flops=8 * CR * Z * B * D, bytes_accessed=2**21, transcendentals=2 * CR * Z * B),
    )(student_feat, teacher_feat, proto_weight)
    gs, gp, loss = pl.pallas_call(
        functools.partial(finish, NB * Z * B),
        out_shape=(
            jax.ShapeDtypeStruct((B, D), F32),
            jax.ShapeDtypeStruct((B, D), F32),
            jax.ShapeDtypeStruct((1, 1), F32),
        ),
        in_specs=[vmem] * 5,
        out_specs=(vmem, vmem, pl.BlockSpec(memory_space=pltpu.SMEM)),
    )(student_feat, proto_weight, gs, gp, loss)
    return gs, gp, loss.reshape(())


def solution(mesh):
    Z = mesh.shape["dp"] // (X * C)
    return jax.shard_map(
        functools.partial(shards, Z),
        mesh=mesh,
        in_specs=(P("dp", None), P("dp", None), P(("proto", "dp"), None)),
        out_specs=(P("dp", None), P(("proto", "dp"), None), P()),
        check_vma=False,
    )
```

```python
import functools
import itertools

import jax
import jax.numpy as jnp
from jax import lax
from jax.experimental import pallas as pl
from jax.experimental.pallas import tpu as pltpu
from jax.sharding import PartitionSpec as P

SWEEPS = 3
X, Y, C = 4, 4, 2
B = 256
D = 256
L = 128
NB = X * C
CR = NB * B
Q = B // Y
NP = 4
SCALE = 1024.0
LOG2E = 1.4426950408889634
EPS = 1e-6
F32, BF16 = jnp.float32, jnp.bfloat16
MESH = pl.DeviceIdType.MESH
NT = (((1,), (1,)), ((), ()))


def inverse_norm(v):
    return lax.rsqrt(jnp.sum(v * v, axis=1, keepdims=True) + EPS)


def unit_back(v, upstream):
    inv = inverse_norm(v)
    u = v * inv
    return (upstream - u * jnp.sum(u * upstream, axis=1, keepdims=True)) * inv


def ring_distance(d, n):
    return min(d, n - d)


def offsets(sizes):
    every = [o for o in itertools.product(*[range(n) for n in sizes]) if any(o)]
    return sorted(every, key=lambda o: -sum(ring_distance(d, n) for d, n in zip(o, sizes)))


def kernel(Z, sf_in, tf_in, pw_in, gs_o, gp_o, loss_o, T, U, PR, K, S, G, cwb, ltb, part, col, colr, stud, studr, wide_row, row, rowr,
           pg, near, nearr, nxt, nxtr, pgr, corer, rss, rsr, gsb, lz, lzr, lx, lxr, cscale, sf, tf, pw, lsem, ssem, rsem, csem, xsem):
    H = ZH = Z // 2
    dp, y = lax.axis_index("dp"), lax.axis_index("proto")
    z, x, c = dp // (X * C), lax.rem(dp // C, X), lax.rem(dp, C)

    def dev(zz, xx, yy, cc):
        return ((zz * X + xx) * C + cc, yy)

    def at_z(d):
        return dev(lax.rem(z + d, Z), x, y, c)

    def at_xyc(o):
        return dev(z, lax.rem(x + o[0], X), lax.rem(y + o[1], Y), lax.rem(c + o[2], C))

    z_offs = [o[0] for o in offsets((Z,))]
    xyc_offs = offsets((X, Y, C))
    xy_offs = offsets((X, Y))
    partner = at_xyc((0, 0, 1))

    loads = [
        pltpu.make_async_copy(src, dst, lsem.at[i]) for i, (src, dst) in enumerate(((pw_in, pw), (tf_in, tf), (sf_in, sf)))
    ]
    for load in loads:
        load.start()
    barrier = pltpu.get_barrier_semaphore()
    for d in z_offs:
        pl.semaphore_signal(barrier, 1, device_id=at_z(d), device_id_type=MESH)
    for o in xyc_offs:
        pl.semaphore_signal(barrier, 1, device_id=at_xyc(o), device_id_type=MESH)

    own = x * C + c

    def unit_into(dst, load, src):
        load.wait()
        v = src[...].astype(F32)
        dst[...] = (v * inverse_norm(v)).astype(BF16)

    unit_into(PR.at[z], loads[0], pw)
    pl.semaphore_wait(barrier, len(z_offs) + len(xyc_offs))

    count = [0]
    sent = []

    def send(src, dst, device):
        i = count[0]
        count[0] += 1
        copy = pltpu.make_async_remote_copy(src, dst, ssem.at[i], rsem.at[i], device_id=device, device_id_type=MESH)
        copy.start()
        sent.append(copy)
        return copy

    def drain():
        for copy in sent:
            copy.wait_send()
        sent.clear()

    def wait_bytes(ref, sem):
        pltpu.make_async_copy(ref, ref, sem).wait()

    def exchange(src, slots, targets, k):
        for i, device in enumerate(targets):
            pltpu.make_async_remote_copy(
                src, slots.at[i], xsem.at[k], csem.at[k], device_id=device, device_id_type=MESH
            ).start()

    def arrive(slots, k):
        wait_bytes(slots, csem.at[k])

    z_targets = [at_z(d) for d in z_offs]
    xyc_targets = [at_xyc(o) for o in xyc_offs]

    up, down = at_z(1), at_z(Z - 1)
    half = B // 2
    lo, hi = pl.ds(0, half), pl.ds(half, half)
    pieces = [pl.ds(i * (B // NP), B // NP) for i in range(NP)]
    ring = [[[send(PR.at[z, rows], PR.at[z, rows], way) for rows in pieces] for way in (up, down)]]

    x_offs = sorted(range(1, X), key=lambda d: -ring_distance(d, X))

    def spread(A):
        return [send(A.at[own], A.at[own], at_xyc((d, 0, 0))) for d in x_offs], [send(A.at[own], A.at[own], partner)]

    def pass_on(A, copies):
        got, to_partner = copies
        for d, copy in zip(x_offs, got):
            copy.wait_recv()
            b = lax.rem(x + X - d, X) * C + c
            to_partner.append(send(A.at[b], A.at[b], partner))

    unit_into(T.at[own], loads[1], tf)
    t_copies = spread(T)
    unit_into(U.at[own], loads[2], sf)

    def ring_step(s):
        step = [[None] * NP, [None] * NP]
        for i, rows in enumerate(pieces):
            for w, (zz, way) in enumerate(((lax.rem(z + Z - s, Z), up), (lax.rem(z + s, Z), down))):
                if ring[s - 1][w][i] is not None:
                    ring[s - 1][w][i].wait_recv()
                    if s + 1 < H or (s < H and (i < NP // 2) == (w == 0)):
                        step[w][i] = send(PR.at[zz, rows], PR.at[zz, rows], way)
        ring.append(step)

    def teacher_block(zz):
        protos = PR[zz]

        def tile(b, acc):
            logits = lax.dot_general(T[b], protos, NT, preferred_element_type=F32)
            e = jnp.exp2(logits * (25.0 * LOG2E))
            K[zz, pl.ds(pl.multiple_of(b * B, B), B)] = e
            return acc + jnp.sum(e.reshape(B // 8, 8, B), axis=0)

        acc = lax.fori_loop(0, NB, tile, jnp.zeros((8, B), F32), unroll=NB)
        sums = jnp.sum(acc, axis=0, keepdims=True)
        for h in range(2):
            col[0, zz // ZH, pl.ds(lax.rem(zz, ZH) * 2 + h, 1)] = sums[:, h * L:(h + 1) * L]

    ring_step(1)
    pass_on(T, t_copies)
    u_copies = spread(U)
    for s in range(2, H):
        ring_step(s)
        if s == 2:
            for copy in t_copies[1]:
                copy.wait_recv()
            teacher_block(z)
        else:
            pass_on(U, u_copies)
        teacher_block(lax.rem(z + Z - s + 1, Z))
        teacher_block(lax.rem(z + s - 1, Z))
    teacher_block(lax.rem(z + Z - H + 1, Z))
    teacher_block(lax.rem(z + H - 1, Z))
    ring_step(H)
    teacher_block(lax.rem(z + H, Z))
    def col_exchange(k, part_of):
        exchange(col.at[k, part_of], colr.at[k, part_of], z_targets, k + part_of * (2 * SWEEPS + 3))

    col_exchange(0, 0)
    col_exchange(0, 1)

    for copy in u_copies[1]:
        copy.wait_recv()

    part[...] = jnp.zeros_like(part)

    def student_block(zz, carry):
        protos = PR[zz]

        def tile(b, carry):
            rows = pl.ds(pl.multiple_of(b * B, B), B)
            scores = lax.dot_general(U[b], protos, NT, preferred_element_type=F32) * (10.0 * LOG2E)
            S[zz, rows] = scores
            e = jnp.exp2(scores)
            part[rows] += e[:, :L] + e[:, L:]
            return carry

        return lax.fori_loop(0, NB, tile, carry, unroll=NB)

    lax.fori_loop(0, Z, student_block, 0)
    drain()
    UT = T
    for b in range(NB):
        UT[b] = U[b].T

    def to_lanes(dst):
        for b in range(NB):
            sums = jnp.sum(part[b * B:(b + 1) * B].T, axis=0, keepdims=True)
            for h in range(2):
                wide_row[h * NB + b:h * NB + b + 1, :] = sums[:, h * L:(h + 1) * L]
        dst[...] = wide_row[...].astype(BF16)

    def to_rows(dst, values):
        for b in range(NB):
            for h in range(2):
                i = h * NB + b
                dst[b * B + h * L:b * B + (h + 1) * L, :] = jnp.broadcast_to(values[i:i + 1], (L, L)).T

    to_lanes(stud)

    R = 128

    def row_pass(part_of, scale):
        wide = [jnp.broadcast_to(scale[i:i + 1], (8, L)) for i in range(2 * ZH)]

        def tile(r, carry):
            rows = pl.ds(pl.multiple_of(r * R, R), R)
            acc = part[rows].reshape(R // 8, 8, L) if part_of else jnp.zeros((R // 8, 8, L), F32)
            for i in range(2 * ZH):
                zz, h = part_of * ZH + i // 2, i % 2
                acc = acc + K[zz, rows, h * L:(h + 1) * L].reshape(R // 8, 8, L) * wide[i][None]
            part[rows] = acc.reshape(R, L)
            return carry

        lax.fori_loop(0, CR // R, tile, 0, unroll=4)

    def col_pass(k, part_of):
        def tile(r, accs):
            rows = pl.ds(pl.multiple_of(r * R, R), R)
            w = cwb[rows].reshape(R // 8, 8, L)
            return tuple(
                accs[i] + jnp.sum(K[part_of * ZH + i // 2, rows, i % 2 * L:(i % 2 + 1) * L].reshape(R // 8, 8, L) * w, axis=0)
                for i in range(2 * ZH)
            )

        accs = lax.fori_loop(0, CR // R, tile, (jnp.zeros((8, L), F32),) * (2 * ZH), unroll=4)
        for i in range(2 * ZH):
            col[k, part_of, i:i + 1] = jnp.sum(accs[i], axis=0, keepdims=True)

    def prepare():
        def tile(b, carry):
            rows = pl.ds(pl.multiple_of(b * B, B), B)
            lt = jnp.concatenate([ltb[rows], ltb[rows]], axis=1)
            acc = jnp.zeros((B, L), F32)
            for zz in range(Z):
                shifted = S[zz, rows] - lt
                S[zz, rows] = jnp.exp2(shifted)
                weighed = K[zz, rows] * cscale[zz:zz + 1] * shifted
                acc = acc + weighed[:, :L] + weighed[:, L:]
            part[rows] = acc
            return carry

        lax.fori_loop(0, NB, tile, 0)

    for k in range(SWEEPS):
        if k > 0:
            for part_of in range(2):
                col_pass(k, part_of)
                col_exchange(k, part_of)
        for part_of in range(2):
            arrive(colr.at[k, part_of], k + part_of * (2 * SWEEPS + 3))
            total = col[k, part_of]
            for i in range(len(z_offs)):
                total = total + colr[k, part_of, i]
            scale = 1.0 / total
            row_pass(part_of, scale)
            if k == SWEEPS - 1:
                for i in range(2 * ZH):
                    zz, h = part_of * ZH + i // 2, i % 2
                    cscale[zz:zz + 1, h * L:(h + 1) * L] = scale[i:i + 1]
        mine, slots = row.at[k], rowr.at[k]
        to_lanes(mine)
        exchange(mine, slots, xyc_targets, SWEEPS + k)
        if k == 0:
            exchange(stud, studr, xyc_targets, 2 * SWEEPS + 2)
        if k == SWEEPS - 1:
            prepare()
            for i in range(SWEEPS):
                for part_of in range(2):
                    wait_bytes(colr.at[i, part_of], xsem.at[i + part_of * (2 * SWEEPS + 3)])
            for i in range(SWEEPS - 1):
                wait_bytes(rowr.at[i], xsem.at[SWEEPS + i])
            wait_bytes(studr, xsem.at[2 * SWEEPS + 2])
        arrive(slots, SWEEPS + k)
        total = mine[...].astype(F32)
        for i in range(len(xyc_offs)):
            total = total + slots[i].astype(F32)
        to_rows(cwb, 1.0 / total)
        if k == 1:
            arrive(studr, 2 * SWEEPS + 2)
            total = stud[...].astype(F32)
            for i in range(len(xyc_offs)):
                total = total + studr[i].astype(F32)
            to_rows(ltb, jnp.log(total) * LOG2E)


    def gradient_block(zz):
        cs = cscale[pl.ds(zz, 1)]

        acc = jnp.zeros((D, B), F32)
        for b in range(NB):
            rows = slice(b * B, (b + 1) * B)
            w = jnp.concatenate([cwb[rows], cwb[rows]], axis=1)
            g = (S[zz, rows] - K[zz, rows] * w * cs).astype(BF16)
            G[zz, rows] = g
            acc = acc + jnp.dot(UT[b], g, preferred_element_type=F32)
        pg[zz] = acc

    def zi(d):
        return lax.rem(z + d, Z)

    steps = []

    def reduce_step(s, j):
        d = H - s + 1
        if j == 0:
            steps.append([[None, None], [None, None]])
        for w, (zz, way) in enumerate(((zi(d), up), (zi(Z - d), down))):
            i = w if j else 1 - w
            rows = (lo, hi)[i]
            if s == 1:
                if j:
                    near[w, rows] = pg[zz, rows].astype(BF16)
                    steps[-1][w][i] = send(near.at[w, rows], nearr.at[w, rows], way)
            elif s == 2:
                total = pg[zz, rows]
                if j:
                    steps[-2][w][i].wait_recv()
                    total = total + nearr[w, rows].astype(F32)
                nxt[w, rows] = total.astype(BF16)
                steps[-1][w][i] = send(nxt.at[w, rows], nxtr.at[w, rows], way)
            else:
                steps[-2][w][i].wait_recv()
                came = nxtr[w, rows].astype(F32) if s == 3 else pgr[w, s - 4, rows]
                pg[zz, rows] += came
                if s <= H:
                    steps[-1][w][i] = send(pg.at[zz, rows], pgr.at[w, s - 3, rows], way)

    gradient_block(zi(H))
    reduce_step(1, 0)
    reduce_step(1, 1)
    for d in range(H - 1, 0, -1):
        gradient_block(zi(d))
        gradient_block(zi(Z - d))
        if d == H - 1:
            reduce_step(2, 0)
    gradient_block(z)
    reduce_step(2, 1)

    lz[...] = jnp.sum((part[...] * cwb[...]).reshape(CR // 8, 8, L), axis=0)
    exchange(lz, lzr, z_targets, 2 * SWEEPS)

    def gu(b, first=0, n=B):
        return K.at[0, pl.ds(pl.multiple_of(b * B + first, n), n)]

    def crop_block(b):
        acc = jnp.dot(G[0, pl.ds(pl.multiple_of(b * B, B), B)], PR[0], preferred_element_type=F32)
        for zz in range(1, Z):
            acc = acc + jnp.dot(G[zz, pl.ds(pl.multiple_of(b * B, B), B)], PR[zz], preferred_element_type=F32)
        gu(b)[...] = acc

    x_order = [*x_offs, 0]
    core_copies = []
    for d in x_order:
        b = lax.rem(x + d, X) * C + (1 - c)
        crop_block(b)
        core_copies.append(send(gu(b), corer.at[lax.rem(x + d, X)], partner))
    reduce_step(3, 0)
    scattered = []
    for d, copy in zip(x_order, core_copies):
        xx = lax.rem(x + d, X)
        b = xx * C + c
        crop_block(b)
        copy.wait_recv()
        total = gu(b)[...] + corer[xx]
        gu(b)[...] = total
        rss[xx] = total.astype(BF16)
        for i, (ox, oy) in enumerate(xy_offs):
            if ox == d:
                q = pl.ds(pl.multiple_of(lax.rem(y + oy, Y) * Q, Q), Q)
                scattered.append(send(rss.at[xx, q], rsr.at[i], at_xyc((ox, oy, 0))))
    reduce_step(3, 1)
    arrive(lzr, 2 * SWEEPS)
    total = lz[...]
    for i in range(len(z_offs)):
        total = total + lzr[i]
    lx[...] = total
    exchange(lx, lxr, xyc_targets, 2 * SWEEPS + 1)
    reduce_step(4, 0)
    reduce_step(4, 1)
    for copy in scattered:
        copy.wait_recv()
    mine = pl.ds(pl.multiple_of(y * Q, Q), Q)
    total = gu(own, y * Q, Q)[...]
    for i in range(len(xy_offs)):
        total = total + rsr[i].astype(F32)
    gsb[mine] = total
    early = list(sent)
    sent.clear()
    y_copies = [send(gsb.at[mine], gsb.at[mine], at_xyc((0, d, 0))) for d in sorted(range(1, Y), key=lambda d: -ring_distance(d, Y))]

    for copy in early:
        copy.wait_send()
    wait_bytes(rowr.at[SWEEPS - 1], xsem.at[2 * SWEEPS - 1])
    wait_bytes(lzr, xsem.at[2 * SWEEPS])
    arrive(lxr, 2 * SWEEPS + 1)
    total = lx[...]
    for i in range(len(xyc_offs)):
        total = total + lxr[i]
    loss_o[...] = total

    reduce_step(H + 1, 0)
    reduce_step(H + 1, 1)
    gp_o[...] = pg[z].T
    for copy in y_copies:
        copy.wait_recv()
    gs_o[...] = gsb[...]

    drain()
    wait_bytes(lxr, xsem.at[2 * SWEEPS + 1])


def finish(crops, sf, pw, gs, gp, loss, gs_o, gp_o, loss_o):
    gs_o[...] = unit_back(sf[...].astype(F32), gs[...] * SCALE)
    gp_o[...] = unit_back(pw[...], gp[...] * SCALE)
    loss_o[0, 0] = jnp.sum(loss[...]) * (-1.0 / (LOG2E * crops))


def shards(Z, student_feat, teacher_feat, proto_weight):
    H = Z // 2
    nx, nz = X * Y * C - 1, Z - 1
    vmem = pl.BlockSpec(memory_space=pltpu.VMEM)
    v = pltpu.VMEM
    copies = 256
    gs, gp, loss = pl.pallas_call(
        functools.partial(kernel, Z),
        out_shape=(
            jax.ShapeDtypeStruct((B, D), F32),
            jax.ShapeDtypeStruct((B, D), F32),
            jax.ShapeDtypeStruct((8, L), F32),
        ),
        in_specs=[pl.BlockSpec(memory_space=pl.ANY)] * 3,
        out_specs=(vmem,) * 3,
        scratch_shapes=[
            v((NB, B, D), BF16), v((NB, B, D), BF16), v((Z, B, D), BF16),
            v((Z, CR, B), F32), v((Z, CR, B), F32), v((Z, CR, B), BF16),
            v((CR, L), F32), v((CR, L), F32), v((CR, L), F32),
            v((SWEEPS, 2, Z, L), F32), v((SWEEPS, 2, nz, Z, L), F32),
            v((2 * NB, L), BF16), v((nx, 2 * NB, L), BF16), v((2 * NB, L), F32),
            v((SWEEPS, 2 * NB, L), BF16), v((SWEEPS, nx, 2 * NB, L), BF16),
            v((Z, D, B), F32), v((2, D, B), BF16), v((2, D, B), BF16), v((2, D, B), BF16), v((2, D, B), BF16),
            v((2, H - 2, D, B), F32), v((X, B, D), F32), v((X, B, D), BF16),
            v((X * Y - 1, Q, D), BF16), v((B, D), F32),
            v((8, L), F32), v((nz, 8, L), F32), v((8, L), F32), v((nx, 8, L), F32), v((Z, B), F32),
            v((B, D), BF16), v((B, D), BF16), v((B, D), F32), pltpu.SemaphoreType.DMA((3,)),
            pltpu.SemaphoreType.DMA((copies,)), pltpu.SemaphoreType.DMA((copies,)),
            pltpu.SemaphoreType.DMA((3 * SWEEPS + 3,)), pltpu.SemaphoreType.DMA((3 * SWEEPS + 3,)),
        ],
        compiler_params=pltpu.CompilerParams(
            collective_id=0, has_side_effects=True, vmem_limit_bytes=62 * 2**20
        ),
        cost_estimate=pl.CostEstimate(flops=8 * CR * Z * B * D, bytes_accessed=2**21, transcendentals=2 * CR * Z * B),
    )(student_feat, teacher_feat, proto_weight)
    gs, gp, loss = pl.pallas_call(
        functools.partial(finish, NB * Z * B),
        out_shape=(
            jax.ShapeDtypeStruct((B, D), F32),
            jax.ShapeDtypeStruct((B, D), F32),
            jax.ShapeDtypeStruct((1, 1), F32),
        ),
        in_specs=[vmem] * 5,
        out_specs=(vmem, vmem, pl.BlockSpec(memory_space=pltpu.SMEM)),
    )(student_feat, proto_weight, gs, gp, loss)
    return gs, gp, loss.reshape(())


def solution(mesh):
    Z = mesh.shape["dp"] // (X * C)
    return jax.shard_map(
        functools.partial(shards, Z),
        mesh=mesh,
        in_specs=(P("dp", None), P("dp", None), P(("proto", "dp"), None)),
        out_specs=(P("dp", None), P(("proto", "dp"), None), P()),
        check_vma=False,
    )
```

```python
import functools
import itertools

import jax
import jax.numpy as jnp
from jax import lax
from jax.experimental import pallas as pl
from jax.experimental.pallas import tpu as pltpu
from jax.sharding import PartitionSpec as P

SWEEPS = 3
X, Y, C = 4, 4, 2
B = 256
D = 256
L = 128
NB = X * C
CR = NB * B
Q = B // Y
NP = 4
SCALE = 1024.0
LOG2E = 1.4426950408889634
EPS = 1e-6
F32, BF16 = jnp.float32, jnp.bfloat16
MESH = pl.DeviceIdType.MESH
NT = (((1,), (1,)), ((), ()))


def inverse_norm(v):
    return lax.rsqrt(jnp.sum(v * v, axis=1, keepdims=True) + EPS)


def unit_back(v, upstream):
    inv = inverse_norm(v)
    u = v * inv
    return (upstream - u * jnp.sum(u * upstream, axis=1, keepdims=True)) * inv


def ring_distance(d, n):
    return min(d, n - d)


def offsets(sizes):
    every = [o for o in itertools.product(*[range(n) for n in sizes]) if any(o)]
    return sorted(every, key=lambda o: -sum(ring_distance(d, n) for d, n in zip(o, sizes)))


def kernel(Z, sf_in, tf_in, pw_in, gs_o, gp_o, loss_o, T, U, PR, K, S, G, cwb, ltb, part, col, colr, stud, studr, wide_row, row, rowr,
           pg, near, nearr, nxt, nxtr, pgr, corer, rss, rsr, gsb, lz, lzr, lx, lxr, cscale, sf, tf, pw, lsem, ssem, rsem, csem, xsem):
    H = ZH = Z // 2
    dp, y = lax.axis_index("dp"), lax.axis_index("proto")
    z, x, c = dp // (X * C), lax.rem(dp // C, X), lax.rem(dp, C)

    def dev(zz, xx, yy, cc):
        return ((zz * X + xx) * C + cc, yy)

    def at_z(d):
        return dev(lax.rem(z + d, Z), x, y, c)

    def at_xyc(o):
        return dev(z, lax.rem(x + o[0], X), lax.rem(y + o[1], Y), lax.rem(c + o[2], C))

    z_offs = [o[0] for o in offsets((Z,))]
    xyc_offs = offsets((X, Y, C))
    xy_offs = offsets((X, Y))
    partner = at_xyc((0, 0, 1))

    loads = [
        pltpu.make_async_copy(src, dst, lsem.at[i]) for i, (src, dst) in enumerate(((pw_in, pw), (tf_in, tf), (sf_in, sf)))
    ]
    for load in loads:
        load.start()
    barrier = pltpu.get_barrier_semaphore()
    for d in z_offs:
        pl.semaphore_signal(barrier, 1, device_id=at_z(d), device_id_type=MESH)
    for o in xyc_offs:
        pl.semaphore_signal(barrier, 1, device_id=at_xyc(o), device_id_type=MESH)

    own = x * C + c

    def unit_into(dst, load, src):
        load.wait()
        v = src[...].astype(F32)
        dst[...] = (v * inverse_norm(v)).astype(BF16)

    unit_into(PR.at[z], loads[0], pw)
    pl.semaphore_wait(barrier, len(z_offs) + len(xyc_offs))

    count = [0]
    sent = []

    def send(src, dst, device):
        i = count[0]
        count[0] += 1
        copy = pltpu.make_async_remote_copy(src, dst, ssem.at[i], rsem.at[i], device_id=device, device_id_type=MESH)
        copy.start()
        sent.append(copy)
        return copy

    def drain():
        for copy in sent:
            copy.wait_send()
        sent.clear()

    def wait_bytes(ref, sem):
        pltpu.make_async_copy(ref, ref, sem).wait()

    def exchange(src, slots, targets, k):
        for i, device in enumerate(targets):
            pltpu.make_async_remote_copy(
                src, slots.at[i], xsem.at[k], csem.at[k], device_id=device, device_id_type=MESH
            ).start()

    def arrive(slots, k):
        wait_bytes(slots, csem.at[k])

    z_targets = [at_z(d) for d in z_offs]
    xyc_targets = [at_xyc(o) for o in xyc_offs]

    up, down = at_z(1), at_z(Z - 1)
    half = B // 2
    lo, hi = pl.ds(0, half), pl.ds(half, half)
    pieces = [pl.ds(i * (B // NP), B // NP) for i in range(NP)]
    ring = [[[send(PR.at[z, rows], PR.at[z, rows], way) for rows in pieces] for way in (up, down)]]

    x_offs = sorted(range(1, X), key=lambda d: -ring_distance(d, X))

    def spread(A):
        return [send(A.at[own], A.at[own], at_xyc((d, 0, 0))) for d in x_offs], [send(A.at[own], A.at[own], partner)]

    def pass_on(A, copies):
        got, to_partner = copies
        for d, copy in zip(x_offs, got):
            copy.wait_recv()
            b = lax.rem(x + X - d, X) * C + c
            to_partner.append(send(A.at[b], A.at[b], partner))

    unit_into(T.at[own], loads[1], tf)
    t_copies = spread(T)
    unit_into(U.at[own], loads[2], sf)

    def ring_step(s):
        step = [[None] * NP, [None] * NP]
        for i, rows in enumerate(pieces):
            for w, (zz, way) in enumerate(((lax.rem(z + Z - s, Z), up), (lax.rem(z + s, Z), down))):
                if ring[s - 1][w][i] is not None:
                    ring[s - 1][w][i].wait_recv()
                    if s + 1 < H or (s < H and (i < NP // 2) == (w == 0)):
                        step[w][i] = send(PR.at[zz, rows], PR.at[zz, rows], way)
        ring.append(step)

    def teacher_block(zz):
        protos = PR[zz]

        def tile(b, acc):
            logits = lax.dot_general(T[b], protos, NT, preferred_element_type=F32)
            e = jnp.exp2(logits * (25.0 * LOG2E))
            K[zz, pl.ds(pl.multiple_of(b * B, B), B)] = e
            return acc + jnp.sum(e.reshape(B // 8, 8, B), axis=0)

        acc = lax.fori_loop(0, NB, tile, jnp.zeros((8, B), F32), unroll=NB)
        sums = jnp.sum(acc, axis=0, keepdims=True)
        for h in range(2):
            col[0, zz // ZH, pl.ds(lax.rem(zz, ZH) * 2 + h, 1)] = sums[:, h * L:(h + 1) * L]

    ring_step(1)
    pass_on(T, t_copies)
    u_copies = spread(U)
    for s in range(2, H):
        ring_step(s)
        if s == 2:
            for copy in t_copies[1]:
                copy.wait_recv()
            teacher_block(z)
        else:
            pass_on(U, u_copies)
        teacher_block(lax.rem(z + Z - s + 1, Z))
        teacher_block(lax.rem(z + s - 1, Z))
    teacher_block(lax.rem(z + Z - H + 1, Z))
    teacher_block(lax.rem(z + H - 1, Z))
    ring_step(H)
    teacher_block(lax.rem(z + H, Z))
    def col_exchange(k, part_of):
        exchange(col.at[k, part_of], colr.at[k, part_of], z_targets, k + part_of * (2 * SWEEPS + 3))

    col_exchange(0, 0)
    col_exchange(0, 1)

    for copy in u_copies[1]:
        copy.wait_recv()

    part[...] = jnp.zeros_like(part)

    def student_block(zz, carry):
        protos = PR[zz]

        def tile(b, carry):
            rows = pl.ds(pl.multiple_of(b * B, B), B)
            scores = lax.dot_general(U[b], protos, NT, preferred_element_type=F32) * (10.0 * LOG2E)
            S[zz, rows] = scores
            e = jnp.exp2(scores)
            part[rows] += e[:, :L] + e[:, L:]
            return carry

        return lax.fori_loop(0, NB, tile, carry, unroll=NB)

    lax.fori_loop(0, Z, student_block, 0)
    drain()
    UT = T
    for b in range(NB):
        UT[b] = U[b].T

    def to_lanes(dst):
        for b in range(NB):
            sums = jnp.sum(part[b * B:(b + 1) * B].T, axis=0, keepdims=True)
            for h in range(2):
                wide_row[h * NB + b:h * NB + b + 1, :] = sums[:, h * L:(h + 1) * L]
        dst[...] = wide_row[...].astype(BF16)

    def to_rows(dst, values):
        for b in range(NB):
            for h in range(2):
                i = h * NB + b
                dst[b * B + h * L:b * B + (h + 1) * L, :] = jnp.broadcast_to(values[i:i + 1], (L, L)).T

    to_lanes(stud)

    R = 128

    def row_pass(part_of, scale):
        wide = [jnp.broadcast_to(scale[i:i + 1], (8, L)) for i in range(2 * ZH)]

        def tile(r, carry):
            rows = pl.ds(pl.multiple_of(r * R, R), R)
            acc = part[rows].reshape(R // 8, 8, L) if part_of else jnp.zeros((R // 8, 8, L), F32)
            for i in range(2 * ZH):
                zz, h = part_of * ZH + i // 2, i % 2
                acc = acc + K[zz, rows, h * L:(h + 1) * L].reshape(R // 8, 8, L) * wide[i][None]
            part[rows] = acc.reshape(R, L)
            return carry

        lax.fori_loop(0, CR // R, tile, 0, unroll=4)

    def col_pass(k, part_of):
        def tile(r, accs):
            rows = pl.ds(pl.multiple_of(r * R, R), R)
            w = cwb[rows].reshape(R // 8, 8, L)
            return tuple(
                accs[i] + jnp.sum(K[part_of * ZH + i // 2, rows, i % 2 * L:(i % 2 + 1) * L].reshape(R // 8, 8, L) * w, axis=0)
                for i in range(2 * ZH)
            )

        accs = lax.fori_loop(0, CR // R, tile, (jnp.zeros((8, L), F32),) * (2 * ZH), unroll=4)
        for i in range(2 * ZH):
            col[k, part_of, i:i + 1] = jnp.sum(accs[i], axis=0, keepdims=True)

    def prepare():
        def tile(b, carry):
            rows = pl.ds(pl.multiple_of(b * B, B), B)
            lt = jnp.concatenate([ltb[rows], ltb[rows]], axis=1)
            acc = jnp.zeros((B, L), F32)
            for zz in range(Z):
                shifted = S[zz, rows] - lt
                S[zz, rows] = jnp.exp2(shifted)
                weighed = K[zz, rows] * cscale[zz:zz + 1] * shifted
                acc = acc + weighed[:, :L] + weighed[:, L:]
            part[rows] = acc
            return carry

        lax.fori_loop(0, NB, tile, 0)

    for k in range(SWEEPS):
        if k > 0:
            for part_of in range(2):
                col_pass(k, part_of)
                col_exchange(k, part_of)
        for part_of in range(2):
            arrive(colr.at[k, part_of], k + part_of * (2 * SWEEPS + 3))
            total = col[k, part_of]
            for i in range(len(z_offs)):
                total = total + colr[k, part_of, i]
            scale = 1.0 / total
            row_pass(part_of, scale)
            if k == SWEEPS - 1:
                for i in range(2 * ZH):
                    zz, h = part_of * ZH + i // 2, i % 2
                    cscale[zz:zz + 1, h * L:(h + 1) * L] = scale[i:i + 1]
        mine, slots = row.at[k], rowr.at[k]
        to_lanes(mine)
        exchange(mine, slots, xyc_targets, SWEEPS + k)
        if k == 0:
            exchange(stud, studr, xyc_targets, 2 * SWEEPS + 2)
        if k == SWEEPS - 1:
            prepare()
            for i in range(SWEEPS):
                for part_of in range(2):
                    wait_bytes(colr.at[i, part_of], xsem.at[i + part_of * (2 * SWEEPS + 3)])
            for i in range(SWEEPS - 1):
                wait_bytes(rowr.at[i], xsem.at[SWEEPS + i])
            wait_bytes(studr, xsem.at[2 * SWEEPS + 2])
        arrive(slots, SWEEPS + k)
        terms = [mine[...].astype(F32)] + [slots[i].astype(F32) for i in range(len(xyc_offs))]
        while len(terms) > 1:
            terms = [sum(terms[i + 1:i + 2], terms[i]) for i in range(0, len(terms), 2)]
        total = terms[0]
        to_rows(cwb, 1.0 / total)
        if k == 1:
            arrive(studr, 2 * SWEEPS + 2)
            total = stud[...].astype(F32)
            for i in range(len(xyc_offs)):
                total = total + studr[i].astype(F32)
            to_rows(ltb, jnp.log(total) * LOG2E)


    def gradient_block(zz):
        cs = cscale[pl.ds(zz, 1)]

        acc = jnp.zeros((D, B), F32)
        for b in range(NB):
            rows = slice(b * B, (b + 1) * B)
            w = jnp.concatenate([cwb[rows], cwb[rows]], axis=1)
            g = (S[zz, rows] - K[zz, rows] * w * cs).astype(BF16)
            G[zz, rows] = g
            acc = acc + jnp.dot(UT[b], g, preferred_element_type=F32)
        pg[zz] = acc

    def zi(d):
        return lax.rem(z + d, Z)

    steps = []

    def reduce_step(s, j):
        d = H - s + 1
        if j == 0:
            steps.append([[None, None], [None, None]])
        for w, (zz, way) in enumerate(((zi(d), up), (zi(Z - d), down))):
            i = w if j else 1 - w
            rows = (lo, hi)[i]
            if s == 1:
                if j:
                    near[w, rows] = pg[zz, rows].astype(BF16)
                    steps[-1][w][i] = send(near.at[w, rows], nearr.at[w, rows], way)
            elif s == 2:
                total = pg[zz, rows]
                if j:
                    steps[-2][w][i].wait_recv()
                    total = total + nearr[w, rows].astype(F32)
                nxt[w, rows] = total.astype(BF16)
                steps[-1][w][i] = send(nxt.at[w, rows], nxtr.at[w, rows], way)
            else:
                steps[-2][w][i].wait_recv()
                came = nxtr[w, rows].astype(F32) if s == 3 else pgr[w, s - 4, rows]
                pg[zz, rows] += came
                if s <= H:
                    steps[-1][w][i] = send(pg.at[zz, rows], pgr.at[w, s - 3, rows], way)

    gradient_block(zi(H))
    reduce_step(1, 0)
    reduce_step(1, 1)
    for d in range(H - 1, 0, -1):
        gradient_block(zi(d))
        gradient_block(zi(Z - d))
        if d == H - 1:
            reduce_step(2, 0)
    gradient_block(z)
    reduce_step(2, 1)

    lz[...] = jnp.sum((part[...] * cwb[...]).reshape(CR // 8, 8, L), axis=0)
    exchange(lz, lzr, z_targets, 2 * SWEEPS)

    def gu(b, first=0, n=B):
        return K.at[0, pl.ds(pl.multiple_of(b * B + first, n), n)]

    def crop_block(b):
        acc = jnp.dot(G[0, pl.ds(pl.multiple_of(b * B, B), B)], PR[0], preferred_element_type=F32)
        for zz in range(1, Z):
            acc = acc + jnp.dot(G[zz, pl.ds(pl.multiple_of(b * B, B), B)], PR[zz], preferred_element_type=F32)
        gu(b)[...] = acc

    x_order = [*x_offs, 0]
    core_copies = []
    for d in x_order:
        b = lax.rem(x + d, X) * C + (1 - c)
        crop_block(b)
        core_copies.append(send(gu(b), corer.at[lax.rem(x + d, X)], partner))
    reduce_step(3, 0)
    scattered = []
    for d, copy in zip(x_order, core_copies):
        xx = lax.rem(x + d, X)
        b = xx * C + c
        crop_block(b)
        copy.wait_recv()
        total = gu(b)[...] + corer[xx]
        gu(b)[...] = total
        rss[xx] = total.astype(BF16)
        for i, (ox, oy) in enumerate(xy_offs):
            if ox == d:
                q = pl.ds(pl.multiple_of(lax.rem(y + oy, Y) * Q, Q), Q)
                scattered.append(send(rss.at[xx, q], rsr.at[i], at_xyc((ox, oy, 0))))
    reduce_step(3, 1)
    arrive(lzr, 2 * SWEEPS)
    total = lz[...]
    for i in range(len(z_offs)):
        total = total + lzr[i]
    lx[...] = total
    exchange(lx, lxr, xyc_targets, 2 * SWEEPS + 1)
    reduce_step(4, 0)
    reduce_step(4, 1)
    for copy in scattered:
        copy.wait_recv()
    mine = pl.ds(pl.multiple_of(y * Q, Q), Q)
    total = gu(own, y * Q, Q)[...]
    for i in range(len(xy_offs)):
        total = total + rsr[i].astype(F32)
    gsb[mine] = total
    early = list(sent)
    sent.clear()
    y_copies = [send(gsb.at[mine], gsb.at[mine], at_xyc((0, d, 0))) for d in sorted(range(1, Y), key=lambda d: -ring_distance(d, Y))]

    for copy in early:
        copy.wait_send()
    wait_bytes(rowr.at[SWEEPS - 1], xsem.at[2 * SWEEPS - 1])
    wait_bytes(lzr, xsem.at[2 * SWEEPS])
    arrive(lxr, 2 * SWEEPS + 1)
    total = lx[...]
    for i in range(len(xyc_offs)):
        total = total + lxr[i]
    loss_o[...] = total

    reduce_step(H + 1, 0)
    reduce_step(H + 1, 1)
    gp_o[...] = pg[z].T
    for copy in y_copies:
        copy.wait_recv()
    gs_o[...] = gsb[...]

    drain()
    wait_bytes(lxr, xsem.at[2 * SWEEPS + 1])


def finish(crops, sf, pw, gs, gp, loss, gs_o, gp_o, loss_o):
    gs_o[...] = unit_back(sf[...].astype(F32), gs[...] * SCALE)
    gp_o[...] = unit_back(pw[...], gp[...] * SCALE)
    loss_o[0, 0] = jnp.sum(loss[...]) * (-1.0 / (LOG2E * crops))


def shards(Z, student_feat, teacher_feat, proto_weight):
    H = Z // 2
    nx, nz = X * Y * C - 1, Z - 1
    vmem = pl.BlockSpec(memory_space=pltpu.VMEM)
    v = pltpu.VMEM
    copies = 256
    gs, gp, loss = pl.pallas_call(
        functools.partial(kernel, Z),
        out_shape=(
            jax.ShapeDtypeStruct((B, D), F32),
            jax.ShapeDtypeStruct((B, D), F32),
            jax.ShapeDtypeStruct((8, L), F32),
        ),
        in_specs=[pl.BlockSpec(memory_space=pl.ANY)] * 3,
        out_specs=(vmem,) * 3,
        scratch_shapes=[
            v((NB, B, D), BF16), v((NB, B, D), BF16), v((Z, B, D), BF16),
            v((Z, CR, B), F32), v((Z, CR, B), F32), v((Z, CR, B), BF16),
            v((CR, L), F32), v((CR, L), F32), v((CR, L), F32),
            v((SWEEPS, 2, Z, L), F32), v((SWEEPS, 2, nz, Z, L), F32),
            v((2 * NB, L), BF16), v((nx, 2 * NB, L), BF16), v((2 * NB, L), F32),
            v((SWEEPS, 2 * NB, L), BF16), v((SWEEPS, nx, 2 * NB, L), BF16),
            v((Z, D, B), F32), v((2, D, B), BF16), v((2, D, B), BF16), v((2, D, B), BF16), v((2, D, B), BF16),
            v((2, H - 2, D, B), F32), v((X, B, D), F32), v((X, B, D), BF16),
            v((X * Y - 1, Q, D), BF16), v((B, D), F32),
            v((8, L), F32), v((nz, 8, L), F32), v((8, L), F32), v((nx, 8, L), F32), v((Z, B), F32),
            v((B, D), BF16), v((B, D), BF16), v((B, D), F32), pltpu.SemaphoreType.DMA((3,)),
            pltpu.SemaphoreType.DMA((copies,)), pltpu.SemaphoreType.DMA((copies,)),
            pltpu.SemaphoreType.DMA((3 * SWEEPS + 3,)), pltpu.SemaphoreType.DMA((3 * SWEEPS + 3,)),
        ],
        compiler_params=pltpu.CompilerParams(
            collective_id=0, has_side_effects=True, vmem_limit_bytes=62 * 2**20
        ),
        cost_estimate=pl.CostEstimate(flops=8 * CR * Z * B * D, bytes_accessed=2**21, transcendentals=2 * CR * Z * B),
    )(student_feat, teacher_feat, proto_weight)
    gs, gp, loss = pl.pallas_call(
        functools.partial(finish, NB * Z * B),
        out_shape=(
            jax.ShapeDtypeStruct((B, D), F32),
            jax.ShapeDtypeStruct((B, D), F32),
            jax.ShapeDtypeStruct((1, 1), F32),
        ),
        in_specs=[vmem] * 5,
        out_specs=(vmem, vmem, pl.BlockSpec(memory_space=pltpu.SMEM)),
    )(student_feat, proto_weight, gs, gp, loss)
    return gs, gp, loss.reshape(())


def solution(mesh):
    Z = mesh.shape["dp"] // (X * C)
    return jax.shard_map(
        functools.partial(shards, Z),
        mesh=mesh,
        in_specs=(P("dp", None), P("dp", None), P(("proto", "dp"), None)),
        out_specs=(P("dp", None), P(("proto", "dp"), None), P()),
        check_vma=False,
    )
```
